32 devices in a mesh: fsdp: 8 (over z, x), ctx: 2 (over y), tp: 2 (over core).
Axes of the slice: x: 2, y: 2, z: 4, core: 2. Of those that a mesh axis runs over, the one named last changes fastest.
Arguments:
- inputs: bfloat16 [8, 448, 1024], P('fsdp', 'ctx'), may hold values from -6 to 6
- encoder_states: bfloat16 [8, 1500, 1024], P('fsdp', 'ctx'), may hold values from -6 to 6
- self_weights: bfloat16 [1024, 3, 1024], P(('fsdp', 'ctx'), None, 'tp'), may hold values from -0.1875 to 0.1875
- self_output: bfloat16 [1024, 1024], P('tp', ('fsdp', 'ctx')), may hold values from -0.5 to 0.5
- cross_query: bfloat16 [1024, 1024], P(('fsdp', 'ctx'), 'tp'), may hold values from -0.1875 to 0.1875
- cross_memory: bfloat16 [1024, 2, 1024], P(('fsdp', 'ctx'), None, 'tp'), may hold values from -0.1875 to 0.1875
- cross_output: bfloat16 [1024, 1024], P('tp', ('fsdp', 'ctx')), may hold values from -0.75 to 0.75
- hidden_in: bfloat16 [1024, 4096], P(('fsdp', 'ctx'), 'tp'), may hold values from -0.1875 to 0.1875
- hidden_out: bfloat16 [4096, 1024], P('tp', ('fsdp', 'ctx')), may hold values from -0.125 to 0.125
- norm_gains: float32 [3, 1024], replicated, may hold values from 0.5 to 1.5
- norm_shifts: float32 [3, 1024], replicated, may hold values from -1.8 to 1.8
- head_biases: float32 [4, 1024], P(None, 'tp'), may hold values from -3 to 3
- output_biases: float32 [3, 1024], replicated, may hold values from -1.8 to 1.8
- hidden_bias: float32 [4096], P('tp'), may hold values from -3 to 3
- cotangent: bfloat16 [8, 448, 1024], P('fsdp', 'ctx'), may hold values from -6 to 6
Outputs:
- layer_output: bfloat16 [8, 448, 1024], P('fsdp', 'ctx')
- grad_inputs: float32 [8, 448, 1024], P('fsdp', 'ctx')
- grad_encoder: float32 [8, 1500, 1024], P('fsdp', 'ctx', 'tp')
- grad_self_weights: float32 [1024, 3, 1024], P(('fsdp', 'ctx'), None, 'tp')
- grad_self_output: float32 [1024, 1024], P('tp', ('fsdp', 'ctx'))
- grad_cross_query: float32 [1024, 1024], P(('fsdp', 'ctx'), 'tp')
- grad_cross_memory: float32 [1024, 2, 1024], P(('fsdp', 'ctx'), None, 'tp')
- grad_cross_output: float32 [1024, 1024], P('tp', ('fsdp', 'ctx'))
- grad_hidden_in: float32 [1024, 4096], P(('fsdp', 'ctx'), 'tp')
- grad_hidden_out: float32 [4096, 1024], P('tp', ('fsdp', 'ctx'))
- grad_norm_gains: float32 [3, 1024], replicated
- grad_norm_shifts: float32 [3, 1024], replicated
- grad_head_biases: float32 [4, 1024], P(None, 'tp')
- grad_output_biases: float32 [3, 1024], replicated
- grad_hidden_bias: float32 [4096], P('tp')
The draws below stay inside these ranges and needn't reach their ends.
All inputs are finite; a program needn't handle non-finite values.
Results may differ from the reference program's by a relative error of at most 0.03.
Values may be sent and summed in bfloat16 or wider, within the bound.
No kernel may reach another device: no remote copies, remote signals or barrier semaphores. Data moves between devices by JAX's collectives and lax.ppermute only.
A program may use at most 128 MiB of HBM per device.

```python
import jax
import jax.numpy as jnp
from jax import lax

D = 1024
HEADS = 16
HEAD_DIM = 64
FF = 4096
LEN = 448
ENC = 1500
CLIPS = 8


def shard_levels(rng, extent, split, smallest, high):
    factor_of, own = 1.0, jax.random.fold_in(rng, 6)
    for position, parts in split:
        steps = jnp.exp(jax.random.uniform(jax.random.fold_in(own, position), (parts,), jnp.float32, smallest / len(split), high / len(split)))
        factor_of = factor_of * jnp.repeat(steps, extent[position] // parts).reshape([-1 if axis == position else 1 for axis in range(len(extent))])
    return factor_of


def scatter_about(rng, dims, spread, bound, cuts=(), dtype=jnp.bfloat16):
    values = jax.random.normal(rng, dims, jnp.float32) * spread
    if len(cuts) > 0:
        values = shard_levels(rng, dims, cuts, -0.22, 0.18) * values
    return jnp.clip(values, min=-bound, max=bound).astype(dtype)


def setup_inputs(seed: int = 0) -> dict:
    keys = jax.random.split(jax.random.key(seed), 16)
    inputs = scatter_about(keys[0], (CLIPS, LEN, D), 1.0, 6.0, ((0, 8), (1, 2)))
    encoder_states = scatter_about(keys[1], (CLIPS, ENC, D), 1.0, 6.0, ((0, 8), (1, 2)))
    self_weights = scatter_about(keys[2], (D, 3, D), D ** -0.5, 0.1875, ((0, 16), (2, 2)))
    self_output = scatter_about(keys[3], (D, D), (D // 8) ** -0.5, 0.5, ((0, 2), (1, 16)))
    cross_query = scatter_about(keys[4], (D, D), D ** -0.5, 0.1875, ((0, 16), (1, 2)))
    cross_memory = scatter_about(keys[5], (D, 2, D), D ** -0.5, 0.1875, ((0, 16), (2, 2)))
    cross_output = scatter_about(keys[6], (D, D), (D // 16) ** -0.5, 0.75, ((0, 2), (1, 16)))
    hidden_in = scatter_about(keys[7], (D, FF), D ** -0.5, 0.1875, ((0, 16), (1, 2)))
    hidden_out = scatter_about(keys[8], (FF, D), (FF // 2) ** -0.5, 0.125, ((0, 2), (1, 16)))
    norm_gains = jnp.clip(1.0 + 0.1 * jax.random.normal(keys[9], (3, D), jnp.float32), 0.5, 1.5)
    norm_shifts = scatter_about(keys[10], (3, D), 0.3, 1.8, (), jnp.float32)
    head_biases = scatter_about(keys[11], (4, D), 0.5, 3.0, ((1, 2),), jnp.float32)
    output_biases = scatter_about(keys[12], (3, D), 0.3, 1.8, (), jnp.float32)
    hidden_bias = scatter_about(keys[13], (FF,), 0.5, 3.0, ((0, 2),), jnp.float32)
    cotangent = scatter_about(keys[14], (CLIPS, LEN, D), 1.0, 6.0, ((0, 8), (1, 2)))
    return dict(inputs=inputs, encoder_states=encoder_states, self_weights=self_weights, self_output=self_output, cross_query=cross_query, cross_memory=cross_memory, cross_output=cross_output, hidden_in=hidden_in, hidden_out=hidden_out, norm_gains=norm_gains, norm_shifts=norm_shifts, head_biases=head_biases, output_biases=output_biases, hidden_bias=hidden_bias, cotangent=cotangent)


@jax.custom_vjp
def low(v):
    return lax.optimization_barrier(v.astype(jnp.bfloat16)).astype(jnp.float32)

@jax.custom_vjp
def low_back(v):
    return v

def low_keep(v):
    return (low(v), None)

def low_pass(kept, grad):
    return (grad,)

def back_keep(v):
    return (v, None)

def back_low(kept, grad):
    return (low(grad),)
low.defvjp(low_keep, low_pass)
low_back.defvjp(back_keep, back_low)
highest = lax.Precision.HIGHEST

def layer_norm(values, scales, shifts):
    row_mean = lax.optimization_barrier(jnp.mean(values, axis=-1, keepdims=True))
    centred = values - row_mean
    variance = lax.optimization_barrier(jnp.mean(centred * centred, axis=-1, keepdims=True))
    return centred * lax.rsqrt(variance + 1e-05) * scales + shifts

def attend(queries, key_rows, value_rows, allowed):
    query_heads = queries.reshape(queries.shape[0], HEADS, HEAD_DIM)
    key_heads = key_rows.reshape(key_rows.shape[0], HEADS, HEAD_DIM)
    value_heads = value_rows.reshape(value_rows.shape[0], HEADS, HEAD_DIM)
    scores = low_back(jnp.einsum('qhe,khe->hqk', query_heads, key_heads, precision=highest) * HEAD_DIM ** (-0.5))
    if allowed is not None:
        scores = jnp.where(allowed, scores, -1e+30)
    weights = low(jax.nn.softmax(scores, axis=-1))
    mixed = jnp.einsum('hqk,khe->qhe', weights, value_heads, precision=highest)
    return low(low_back(mixed.reshape(queries.shape[0], D)))

def clip_forward(params, clip_inputs, clip_frames):
    self_weights, self_output, cross_query, cross_memory, cross_output, hidden_in, hidden_out, norm_gains, norm_shifts, head_biases, output_biases, hidden_bias = params
    normed_one = low(layer_norm(clip_inputs, norm_gains[0], norm_shifts[0]))
    projected = jnp.einsum('td,dka->tka', normed_one, self_weights, precision=highest)
    queries = low(low_back(projected[:, 0] + head_biases[0]))
    self_keys = low(low_back(projected[:, 1]))
    self_values = low(low_back(projected[:, 2] + head_biases[1]))
    positions = jnp.arange(LEN)
    allowed = positions[:, None] >= positions[None, :]
    self_mixed = attend(queries, self_keys, self_values, allowed)
    after_self = clip_inputs + low_back(jnp.dot(self_mixed, self_output, precision=highest) + output_biases[0])
    normed_two = low(layer_norm(after_self, norm_gains[1], norm_shifts[1]))
    cross_queries = low(low_back(jnp.dot(normed_two, cross_query, precision=highest) + head_biases[2]))
    frame_proj = jnp.einsum('fd,dka->fka', clip_frames, cross_memory, precision=highest)
    frame_keys = low(low_back(frame_proj[:, 0]))
    frame_values = low(low_back(frame_proj[:, 1] + head_biases[3]))
    cross_mixed = attend(cross_queries, frame_keys, frame_values, None)
    after_cross = after_self + low_back(jnp.dot(cross_mixed, cross_output, precision=highest) + output_biases[1])
    normed_three = low(layer_norm(after_cross, norm_gains[2], norm_shifts[2]))
    pre_gelu = low_back(jnp.dot(normed_three, hidden_in, precision=highest) + hidden_bias)
    activated = low(jax.nn.gelu(pre_gelu, approximate=False))
    return after_cross + low_back(jnp.dot(activated, hidden_out, precision=highest) + output_biases[2])

def reference(inputs, encoder_states, self_weights, self_output, cross_query, cross_memory, cross_output, hidden_in, hidden_out, norm_gains, norm_shifts, head_biases, output_biases, hidden_bias, cotangent):
    params = (self_weights.astype(jnp.float32), self_output.astype(jnp.float32), cross_query.astype(jnp.float32), cross_memory.astype(jnp.float32), cross_output.astype(jnp.float32), hidden_in.astype(jnp.float32), hidden_out.astype(jnp.float32), norm_gains.astype(jnp.float32), norm_shifts.astype(jnp.float32), head_biases.astype(jnp.float32), output_biases.astype(jnp.float32), hidden_bias.astype(jnp.float32))
    stream = inputs.astype(jnp.float32)
    frames = encoder_states.astype(jnp.float32)

    def whole_layer(layer_params, layer_inputs, layer_frames):
        per_clip = jax.checkpoint(lambda clip_pair: clip_forward(layer_params, clip_pair[0], clip_pair[1]))
        return lax.map(per_clip, (layer_inputs, layer_frames))
    output, pullback = jax.vjp(whole_layer, params, stream, frames)
    grad_params, grad_inputs, grad_encoder = pullback(cotangent.astype(jnp.float32))
    return (output.astype(jnp.bfloat16), grad_inputs, grad_encoder, grad_params[0], grad_params[1], grad_params[2], grad_params[3], grad_params[4], grad_params[5], grad_params[6], grad_params[7], grad_params[8], grad_params[9], grad_params[10], grad_params[11])
```

```python
import jax
import jax.numpy as jnp
from jax import lax
from jax.sharding import PartitionSpec as P

HEAD_DIM = 64
SCALING = HEAD_DIM ** (-0.5)
F32 = jnp.float32
BF16 = jnp.bfloat16


def dot(left, right, left_dim, right_dim):
    return lax.dot_general(
        left, right, (((left_dim,), (right_dim,)), ((), ())), preferred_element_type=F32
    )


def layer_norm(values, scales, shifts):
    row_mean = jnp.mean(values, axis=-1, keepdims=True)
    centred = values - row_mean
    variance = jnp.mean(centred * centred, axis=-1, keepdims=True)
    inverse = lax.rsqrt(variance + 1e-05)
    hat = centred * inverse
    return hat * scales + shifts, hat, inverse


def norm_back(hat, inverse, scales, incoming):
    scaled = incoming * scales
    return (
        scaled
        - jnp.mean(scaled, axis=-1, keepdims=True)
        - hat * jnp.mean(scaled * hat, axis=-1, keepdims=True)
    ) * inverse


def heads_of(values):
    return values.reshape(values.shape[0], -1, HEAD_DIM)


def masked_scores(queries, keys, allowed):
    scores = jnp.einsum("qhe,khe->hqk", queries, keys, preferred_element_type=F32) * SCALING
    if allowed is not None:
        scores = jnp.where(allowed, scores, -1e30)
    return scores


def attend_forward(queries, keys, values, allowed):
    queries, keys, values = heads_of(queries), heads_of(keys), heads_of(values)
    scores = masked_scores(queries, keys, allowed)
    row_max = jnp.max(scores, axis=-1, keepdims=True)
    totals = row_max + jnp.log(jnp.sum(jnp.exp(scores - row_max), axis=-1, keepdims=True))
    weights = jnp.exp(scores - totals).astype(BF16)
    mixed = jnp.einsum("hqk,khe->qhe", weights, values, preferred_element_type=F32)
    return mixed.reshape(mixed.shape[0], -1).astype(BF16), totals


def attend_backward(queries, keys, values, allowed, totals, grad_mixed):
    queries, keys, values = heads_of(queries), heads_of(keys), heads_of(values)
    grad_mixed = heads_of(grad_mixed)
    probabilities = jnp.exp(masked_scores(queries, keys, allowed) - totals)
    weights = probabilities.astype(BF16)
    grad_weights = jnp.einsum("qhe,khe->hqk", grad_mixed, values, preferred_element_type=F32)
    row_dot = jnp.sum(grad_weights * probabilities, axis=-1, keepdims=True)
    grad_scores = (probabilities * (grad_weights - row_dot)).astype(BF16)
    grad_queries = jnp.einsum("hqk,khe->qhe", grad_scores, keys, preferred_element_type=F32)
    grad_keys = jnp.einsum("hqk,qhe->khe", grad_scores, queries, preferred_element_type=F32)
    grad_values = jnp.einsum("hqk,qhe->khe", weights, grad_mixed, preferred_element_type=F32)

    def merged(values):
        return values.reshape(values.shape[0], -1)

    return (
        merged(grad_queries * SCALING).astype(BF16),
        merged(grad_keys * SCALING).astype(BF16),
        merged(grad_values).astype(BF16),
    )


def build(fsdp, ctx, tp):
    assert ctx == 2
    ring = list(range(0, fsdp, 2)) + list(range(fsdp - 1, 0, -2)) if fsdp > 1 else [0]
    onward = [(ring[i], ring[(i + 1) % fsdp]) for i in range(fsdp)]
    backward_ring = [(b, a) for a, b in onward]
    swap = [(0, 1), (1, 0)]

    def ring_place(index):
        return jnp.where(index % 2 == 0, index // 2, fsdp - 1 - index // 2)

    def ring_index(place):
        place = place % fsdp
        return jnp.where(2 * place < fsdp, 2 * place, 2 * fsdp - 1 - 2 * place)

    def ctx_swap(values):
        return lax.ppermute(values, "ctx", swap)

    def tp_swap(values):
        return lax.ppermute(values, "tp", swap)

    def ordered(first, second, index, axis):
        return jnp.where(
            index == 0,
            jnp.concatenate((first, second), axis=axis),
            jnp.concatenate((second, first), axis=axis),
        )

    def per_device(
        inputs,
        encoder_states,
        self_weights,
        self_output,
        cross_query,
        cross_memory,
        cross_output,
        hidden_in,
        hidden_out,
        norm_gains,
        norm_shifts,
        head_biases,
        output_biases,
        hidden_bias,
        cotangent,
    ):
        f, c, t = lax.axis_index("fsdp"), lax.axis_index("ctx"), lax.axis_index("tp")
        place = ring_place(f)
        rows, width = inputs.shape[1], inputs.shape[2]
        part = rows // tp
        shard = self_weights.shape[0]

        def tp_gather(values):
            if tp == 2:
                return jnp.stack((values, tp_swap(values)), axis=1)
            return lax.all_gather(values, "tp", axis=1)

        def tp_scatter(values):
            if tp == 2:
                return values[:, 0] + tp_swap(values[:, 1].astype(BF16)).astype(F32)
            return lax.psum_scatter(
                values.astype(BF16), "tp", scatter_dimension=1, tiled=False
            ).astype(F32)

        def group_gather(own):
            both = jnp.stack((own, ctx_swap(own)), axis=0)
            return tp_gather(both).reshape(2 * rows, -1)

        def group_scatter(partial):
            mine = tp_scatter(partial.reshape(2, tp, part, -1))
            return mine[0] + ctx_swap(mine[1].astype(BF16)).astype(F32)

        def own_part(values):
            return lax.dynamic_slice_in_dim(values, t * part, part, axis=0)

        def to_relative(values):
            if tp == 2:
                return ordered(values[:part], values[part:], t, 0)
            return values

        def chip_rows(own):
            if tp == 2:
                return ordered(own, tp_swap(own), t, 0)
            return lax.all_gather(own, "tp", axis=0, tiled=True)

        def all_tokens(values):
            other = ctx_swap(own_part(values))
            other = tp_gather(other[None]).reshape(rows, -1)
            return jnp.concatenate((to_relative(values), other), axis=0)

        def positions():
            j = jnp.arange(2 * rows, dtype=jnp.int32)
            jc, jt, i = j // rows, (j // part) % tp, j % part
            if tp == 2:
                jt = jt ^ t
            return (jc ^ c) * rows + jt * part + i

        def quarters(weight):
            split = weight.reshape(shard, weight.shape[1], ctx, -1)
            mine = lax.dynamic_index_in_dim(split, c, 2, keepdims=False).reshape(shard, -1)
            other = lax.dynamic_index_in_dim(split, 1 - c, 2, keepdims=False).reshape(shard, -1)
            return mine, other

        def ring_gather(weights):
            pairs = [quarters(weight) for weight in weights]
            mine = jnp.concatenate([pair[0] for pair in pairs], axis=1)
            other = ctx_swap(jnp.concatenate([pair[1] for pair in pairs], axis=1))
            full = jnp.zeros((fsdp, ctx, shard, mine.shape[1]), BF16)
            for step in range(fsdp):
                if step > 0:
                    mine = lax.ppermute(mine, "fsdp", onward)
                    other = lax.ppermute(other, "fsdp", backward_ring)
                full = lax.dynamic_update_slice(
                    full, mine[None, None], (ring_index(place + fsdp - step), c, 0, 0)
                )
                full = lax.dynamic_update_slice(
                    full, other[None, None], (ring_index(place + step), 1 - c, 0, 0)
                )
            return full.reshape(width, -1)

        def ring_scatter(gradient, spans):
            blocks = gradient.astype(BF16).reshape(fsdp, ctx, shard, -1)

            def block(where, half):
                return lax.dynamic_slice(
                    blocks, (ring_index(where), half, 0, 0), (1, 1) + blocks.shape[2:]
                )[0, 0]

            theirs = block(place + fsdp - 1, 1 - c)
            mine = block(place + 1, c)
            for step in range(1, fsdp):
                theirs = (
                    lax.ppermute(theirs, "fsdp", onward).astype(F32)
                    + block(place + 2 * fsdp - 1 - step, 1 - c).astype(F32)
                ).astype(BF16)
                mine = (
                    lax.ppermute(mine, "fsdp", backward_ring).astype(F32)
                    + block(place + 1 + step, c).astype(F32)
                ).astype(BF16)
            theirs = ctx_swap(theirs)
            results, start = [], 0
            for count, size in spans:
                stop = start + count * size
                a = mine[:, start:stop].reshape(shard, count, 1, size)
                b = theirs[:, start:stop].reshape(shard, count, 1, size)
                results.append(ordered(a, b, c, 2).reshape(shard, count, -1).astype(F32))
                start = stop
            return results

        q_self = self_weights.shape[2] // ctx
        q_hidden = hidden_in.shape[1] // ctx
        w_qkv = ring_gather([self_weights])
        w_mid = ring_gather(
            [
                cross_memory,
                self_output.T[:, None],
                cross_query[:, None],
                cross_output.T[:, None],
            ]
        )
        w_in = ring_gather([hidden_in[:, None]])
        w_out = ring_gather([hidden_out.T[:, None]])
        w_memory = w_mid[:, : 2 * q_self]
        w_self_out = w_mid[:, 2 * q_self : 3 * q_self]
        w_query = w_mid[:, 3 * q_self : 4 * q_self]
        w_cross_out = w_mid[:, 4 * q_self :]

        def my_bias(bias):
            return lax.dynamic_index_in_dim(
                bias.reshape(bias.shape[:-1] + (ctx, -1)), c, bias.ndim - 1, keepdims=False
            )

        head_bias = my_bias(head_biases)
        hidden_own_bias = my_bias(hidden_bias)

        tokens = all_tokens(inputs[0]).astype(F32)
        frames_here = encoder_states[0]
        if tp == 2:
            half = width // 2
            piece = ctx_swap(lax.dynamic_slice_in_dim(frames_here, t * half, half, axis=1))
            frames_there = ordered(piece, tp_swap(piece), t, 1)
        else:
            piece = ctx_swap(
                lax.dynamic_slice_in_dim(frames_here, t * (width // tp), width // tp, axis=1)
            )
            frames_there = lax.all_gather(piece, "tp", axis=1, tiled=True)
        cot_all = all_tokens(cotangent[0])
        cot_own = own_part(cotangent[0]).astype(F32)
        stream_own = own_part(inputs[0]).astype(F32)

        normed_one, hat_one, inverse_one = layer_norm(tokens, norm_gains[0], norm_shifts[0])
        normed_one = normed_one.astype(BF16)
        projected = dot(normed_one, w_qkv, 1, 0)
        queries = (projected[:, :q_self] + head_bias[0]).astype(BF16)
        self_keys = projected[:, q_self : 2 * q_self].astype(BF16)
        self_values = (projected[:, 2 * q_self :] + head_bias[1]).astype(BF16)
        place_of = positions()
        allowed = place_of[:, None] >= place_of[None, :]
        self_mixed, self_totals = attend_forward(queries, self_keys, self_values, allowed)
        after_self = stream_own + (
            group_scatter(dot(self_mixed, w_self_out, 1, 1)) + output_biases[0]
        )
        normed_two, hat_two, inverse_two = layer_norm(after_self, norm_gains[1], norm_shifts[1])
        normed_two = group_gather(normed_two.astype(BF16))
        cross_queries = (dot(normed_two, w_query, 1, 0) + head_bias[2]).astype(BF16)

        memory_bias = jnp.concatenate((jnp.zeros((q_self,), F32), head_bias[3]))

        frames = jnp.concatenate((frames_here, frames_there), axis=0)
        frame_proj = (dot(frames, w_memory, 1, 0) + memory_bias).astype(BF16)
        frame_keys, frame_values = frame_proj[:, :q_self], frame_proj[:, q_self:]
        cross_mixed, cross_totals = attend_forward(cross_queries, frame_keys, frame_values, None)
        after_cross = after_self + (
            group_scatter(dot(cross_mixed, w_cross_out, 1, 1)) + output_biases[1]
        )
        normed_three, hat_three, inverse_three = layer_norm(
            after_cross, norm_gains[2], norm_shifts[2]
        )
        normed_three = group_gather(normed_three.astype(BF16))
        pre_gelu = dot(normed_three, w_in, 1, 0) + hidden_own_bias
        cdf = 0.5 * (1.0 + lax.erf(pre_gelu * (0.5**0.5)))
        activated = (pre_gelu * cdf).astype(BF16)
        slope = cdf + pre_gelu * jnp.exp(-0.5 * pre_gelu * pre_gelu) * 0.3989422804014327
        hidden_total = group_scatter(dot(activated, w_out, 1, 1))
        output_own = (after_cross + (hidden_total + output_biases[2])).astype(BF16)
        layer_output = chip_rows(output_own)[None]

        grad_pre_wide = dot(cot_all, w_out, 1, 0) * slope
        grad_pre = grad_pre_wide.astype(BF16)
        grad_three = group_scatter(dot(grad_pre, w_in, 1, 1))
        grad_out_t = dot(cot_all, activated, 0, 0)
        grad_in = dot(normed_three, grad_pre, 0, 0)
        (grad_hidden_out,) = ring_scatter(grad_out_t, [(1, q_hidden)])
        (grad_hidden_in,) = ring_scatter(grad_in, [(1, q_hidden)])
        grad_after_cross = cot_own + norm_back(
            hat_three, inverse_three, norm_gains[2], grad_three
        )
        grad_cross_own = grad_after_cross.astype(BF16)
        grad_cross = group_gather(grad_cross_own)

        grad_cross_mixed = dot(grad_cross, w_cross_out, 1, 0).astype(BF16)
        grad_cross_queries, grad_fkeys, grad_fvalues = attend_backward(
            cross_queries, frame_keys, frame_values, None, cross_totals, grad_cross_mixed
        )
        grad_two = group_scatter(dot(grad_cross_queries, w_query, 1, 1))
        grad_frames = jnp.concatenate((grad_fkeys, grad_fvalues), axis=1)
        grad_memory = dot(frames, grad_frames, 0, 0)
        grad_cross_out = dot(grad_cross, cross_mixed, 0, 0)
        grad_query = dot(normed_two, grad_cross_queries, 0, 0)
        encoder_part = dot(grad_frames, w_memory, 1, 1)
        if tp == 2:
            half = width // 2
            keep = lax.dynamic_slice_in_dim(encoder_part, t * half, half, axis=1)
            give = lax.dynamic_slice_in_dim(encoder_part, (1 - t) * half, half, axis=1)
            encoder_sum = keep + tp_swap(give.astype(BF16)).astype(F32)
        else:
            encoder_sum = lax.psum_scatter(
                encoder_part.astype(BF16), "tp", scatter_dimension=1, tiled=True
            ).astype(F32)
        frame_rows = frames_here.shape[0]
        grad_encoder = (
            encoder_sum[:frame_rows]
            + ctx_swap(encoder_sum[frame_rows:].astype(BF16)).astype(F32)
        )[None]

        grad_after_self = grad_after_cross + norm_back(
            hat_two, inverse_two, norm_gains[1], grad_two
        )
        grad_self_own = grad_after_self.astype(BF16)
        grad_self = group_gather(grad_self_own)

        grad_self_mixed = dot(grad_self, w_self_out, 1, 0).astype(BF16)
        grad_queries, grad_keys, grad_values = attend_backward(
            queries, self_keys, self_values, allowed, self_totals, grad_self_mixed
        )
        grad_projected = jnp.concatenate((grad_queries, grad_keys, grad_values), axis=1)
        grad_qkv = dot(normed_one, grad_projected, 0, 0)
        grad_self_out = dot(grad_self, self_mixed, 0, 0)
        grad_one_part = dot(grad_projected, w_qkv, 1, 1)
        grad_one = group_scatter(grad_one_part)
        grad_inputs = chip_rows(
            grad_after_self
            + norm_back(own_rows(hat_one, part), own_rows(inverse_one, part), norm_gains[0], grad_one)
            if tp == 2
            else grad_after_self
            + norm_back(own_part(hat_one), own_part(inverse_one), norm_gains[0], grad_one)
        )[None]
        grad_memory, grad_cross_output, grad_cross_query, grad_self_output = ring_scatter(
            jnp.concatenate((grad_memory, grad_cross_out, grad_query, grad_self_out), axis=1),
            [(2, q_self), (1, q_self), (1, q_self), (1, q_self)],
        )
        (grad_self_weights,) = ring_scatter(grad_qkv, [(3, q_self)])

        def column_sum(values):
            return jnp.sum(values.astype(F32), axis=0)

        wide = jnp.stack(
            (
                column_sum(grad_one_part * hat_one),
                column_sum(hat_two * grad_two),
                column_sum(hat_three * grad_three),
                column_sum(grad_one_part),
                column_sum(grad_two),
                column_sum(grad_three),
                column_sum(grad_self_own),
                column_sum(grad_cross_own),
                column_sum(cot_own),
            )
        )
        narrow = jnp.concatenate(
            (
                column_sum(grad_queries),
                column_sum(grad_values),
                column_sum(grad_cross_queries),
                column_sum(grad_fvalues),
                column_sum(grad_pre),
            )
        )
        if tp == 2:
            wide = wide + tp_swap(wide)
        else:
            wide = lax.psum(wide, "tp")
        wide = wide + ctx_swap(wide)
        small = jnp.concatenate((wide.reshape(-1), narrow))
        hop = 1
        while hop < fsdp:
            small = small + lax.ppermute(small, "fsdp", [(i, i ^ hop) for i in range(fsdp)])
            hop *= 2
        wide = small[: 9 * width].reshape(9, width)
        narrow = small[9 * width :]
        both = ordered(narrow[None], ctx_swap(narrow)[None], c, 0)
        grad_head = both[:, : 4 * q_self].reshape(ctx, 4, q_self)
        grad_head = jnp.transpose(grad_head, (1, 0, 2)).reshape(4, -1)
        grad_hidden_bias = both[:, 4 * q_self :].reshape(-1)
        return (
            layer_output,
            grad_inputs,
            grad_encoder,
            grad_self_weights,
            grad_self_output[:, 0].T,
            grad_cross_query[:, 0],
            grad_memory,
            grad_cross_output[:, 0].T,
            grad_hidden_in[:, 0],
            grad_hidden_out[:, 0].T,
            wide[0:3],
            wide[3:6],
            grad_head,
            wide[6:9],
            grad_hidden_bias,
        )

    def own_rows(values, part):
        return values[:part]

    return per_device


def solution(mesh):
    in_specs = (
        P("fsdp", "ctx", None),
        P("fsdp", "ctx", None),
        P(("fsdp", "ctx"), None, "tp"),
        P("tp", ("fsdp", "ctx")),
        P(("fsdp", "ctx"), "tp"),
        P(("fsdp", "ctx"), None, "tp"),
        P("tp", ("fsdp", "ctx")),
        P(("fsdp", "ctx"), "tp"),
        P("tp", ("fsdp", "ctx")),
        P(),
        P(),
        P(None, "tp"),
        P(),
        P("tp"),
        P("fsdp", "ctx", None),
    )
    out_specs = (
        P("fsdp", "ctx", None),
        P("fsdp", "ctx", None),
        P("fsdp", "ctx", "tp"),
        P(("fsdp", "ctx"), None, "tp"),
        P("tp", ("fsdp", "ctx")),
        P(("fsdp", "ctx"), "tp"),
        P(("fsdp", "ctx"), None, "tp"),
        P("tp", ("fsdp", "ctx")),
        P(("fsdp", "ctx"), "tp"),
        P("tp", ("fsdp", "ctx")),
        P(),
        P(),
        P(None, "tp"),
        P(),
        P("tp"),
    )
    per_device = build(mesh.shape["fsdp"], mesh.shape["ctx"], mesh.shape["tp"])
    return jax.shard_map(
        per_device, mesh=mesh, in_specs=in_specs, out_specs=out_specs, check_vma=False
    )
```

```python
import functools

import jax
import jax.numpy as jnp
from jax import lax
from jax.experimental import pallas as pl
from jax.experimental.pallas import tpu as pltpu
from jax.sharding import PartitionSpec as P

HEAD_DIM = 64
SCALING = HEAD_DIM ** (-0.5)
F32 = jnp.float32
BF16 = jnp.bfloat16


def key_tile(total):
    return 256 if total % 256 == 0 else total

def mm(left, right, left_dim, right_dim):
    return lax.dot_general(
        left, right, (((left_dim,), (right_dim,)), ((), ())), preferred_element_type=F32
    )

def only_head(values, head, group):
    if group == HEAD_DIM: return values
    lane = lax.broadcasted_iota(jnp.int32, values.shape, 1)
    return jnp.where(lane // HEAD_DIM == head, values, jnp.zeros_like(values))

def visible(tile, queries, start, used, half, key_place, query_place):
    if key_place is not None:
        return key_place[start:start+tile, :] <= query_place[...]
    row = start % half
    if row + tile > used:
        return row + lax.broadcasted_iota(jnp.int32, (tile, queries), 0) < used
    return None

def forward_kernel(used, half, causal, *refs):
    if causal:
        kp, qp, q_ref, k_ref, v_ref, mixed_ref, exact_ref, totals_ref = refs
    else:
        q_ref, k_ref, v_ref, mixed_ref, exact_ref, totals_ref = refs; kp = qp = None
    keys, group = k_ref.shape; queries = q_ref.shape[0]; tile = key_tile(keys)
    heads = group // HEAD_DIM
    q = (q_ref[...].astype(F32) * SCALING).astype(BF16)
    starts = range(0, keys, tile)
    qs = [only_head(q, h, group) for h in range(heads)]
    scores = [[None] * len(starts) for _ in range(heads)]
    tops = [None] * heads
    for i, start in enumerate(starts):
        ok = visible(tile, queries, start, used, half, kp, qp)
        for h in range(heads):
            s = mm(k_ref[start:start+tile, :], qs[h], 1, 1)
            if ok is not None: s = jnp.where(ok, s, -1e30)
            m = jnp.max(s, axis=0, keepdims=True)
            tops[h] = m if tops[h] is None else jnp.maximum(tops[h], m)
            scores[h][i] = s
    totals = [None] * heads; accs = [None] * heads
    for i, start in enumerate(starts):
        for h in range(heads):
            e = jnp.exp(scores[h][i] - tops[h])
            es = jnp.sum(e, axis=0, keepdims=True)
            o = mm(v_ref[start:start+tile, :], e.astype(BF16), 0, 0)
            totals[h] = es if totals[h] is None else totals[h] + es
            accs[h] = o if accs[h] is None else accs[h] + o
    for h in range(heads):
        rows = slice(h*HEAD_DIM, (h+1)*HEAD_DIM)
        exact_ref[rows, :] = accs[h][rows, :] * (1.0/totals[h])
        totals_ref[0, h:h+1, :] = tops[h] + jnp.log(totals[h])
    mixed_ref[...] = exact_ref[...].T.astype(BF16)

def backward_kernel(used, half, causal, *refs):
    if causal:
        kp, qp, q_ref, k_ref, v_ref, g_ref, exact_ref, totals_ref, dq_ref, dk_ref, dv_ref = refs
    else:
        q_ref, k_ref, v_ref, g_ref, exact_ref, totals_ref, dq_ref, dk_ref, dv_ref = refs; kp = qp = None
    keys, group = k_ref.shape; queries = q_ref.shape[0]; tile = key_tile(keys)
    heads = group // HEAD_DIM
    q = (q_ref[...].astype(F32) * SCALING).astype(BF16)
    g = g_ref[...]
    both = exact_ref[...] * g.astype(F32).T
    qs = [only_head(q, h, group) for h in range(heads)]
    gs = [only_head(g, h, group) for h in range(heads)]
    dots = [jnp.sum(both[h*HEAD_DIM:(h+1)*HEAD_DIM, :], axis=0, keepdims=True) for h in range(heads)]
    dqs = [None]*heads
    for start in range(0, keys, tile):
        k = k_ref[start:start+tile, :]; v = v_ref[start:start+tile, :]
        ok = visible(tile, queries, start, used, half, kp, qp)
        dk = dv = None
        for h in range(heads):
            s = mm(k, qs[h], 1, 1)
            if ok is not None: s = jnp.where(ok, s, -1e30)
            p = jnp.exp(s - totals_ref[0, h:h+1, :])
            dp = mm(v, gs[h], 1, 1)
            ds = (p * (dp - dots[h])).astype(BF16)
            a = mm(ds, qs[h], 1, 0); b = mm(p.astype(BF16), gs[h], 1, 0)
            dk = a if dk is None else dk + a
            dv = b if dv is None else dv + b
            c = mm(k, ds, 0, 0)
            dqs[h] = c if dqs[h] is None else dqs[h] + c
        dk_ref[start:start+tile, :] = dk.astype(BF16)
        dv_ref[start:start+tile, :] = dv.astype(BF16)
    full = jnp.concatenate([dqs[h][h*HEAD_DIM:(h+1)*HEAD_DIM, :] for h in range(heads)], axis=0)
    dq_ref[...] = (full.T * SCALING).astype(BF16)

def attend_forward(q, k, v, used, half, places=None):
    queries, width = q.shape; keys = k.shape[0]; group = min(128, width); n = width//group
    col = lambda rows: pl.BlockSpec((rows, group), lambda i: (0, i))
    fixed = lambda shape: pl.BlockSpec(shape, lambda i: (0, 0))
    extra = [] if places is None else list(places)
    return pl.pallas_call(
        functools.partial(forward_kernel, used, half, places is not None),
        grid=(n,),
        in_specs=[fixed(p.shape) for p in extra]+[col(queries), col(keys), col(keys)],
        out_specs=[col(queries), pl.BlockSpec((group, queries), lambda i: (i, 0)), pl.BlockSpec((1, group//HEAD_DIM, queries), lambda i: (i,0,0))],
        out_shape=[jax.ShapeDtypeStruct((queries,width),BF16), jax.ShapeDtypeStruct((width,queries),F32), jax.ShapeDtypeStruct((n,group//HEAD_DIM,queries),F32)],
        compiler_params=pltpu.CompilerParams(vmem_limit_bytes=40*2**20),
    )(*extra, q, k, v)

def attend_backward(q, k, v, g, exact, totals, used, half, places=None):
    queries, width = q.shape; keys = k.shape[0]; group = min(128, width); n = width//group
    col = lambda rows: pl.BlockSpec((rows, group), lambda i: (0, i))
    fixed = lambda shape: pl.BlockSpec(shape, lambda i: (0, 0))
    extra = [] if places is None else list(places)
    return pl.pallas_call(
        functools.partial(backward_kernel, used, half, places is not None),
        grid=(n,),
        in_specs=[fixed(p.shape) for p in extra]+[col(queries), col(keys), col(keys), col(queries), pl.BlockSpec((group, queries), lambda i: (i, 0)), pl.BlockSpec((1, group//HEAD_DIM, queries), lambda i: (i,0,0))],
        out_specs=[col(queries), col(keys), col(keys)],
        out_shape=[jax.ShapeDtypeStruct((queries,width),BF16), jax.ShapeDtypeStruct((keys,width),BF16), jax.ShapeDtypeStruct((keys,width),BF16)],
        compiler_params=pltpu.CompilerParams(vmem_limit_bytes=40*2**20),
    )(*extra, q, k, v, g, exact, totals)


def weight_grads_kernel(count, *refs):
    out_ref, start = refs[2 * count], 0
    for i in range(count):
        left, right = refs[i], refs[count + i]
        stop = start + right.shape[1]
        out_ref[:, start:stop] = mm(left[...], right[...], 0, 0).astype(BF16)
        start = stop


def weight_grads(pairs):
    width = pairs[0][0].shape[1]
    tile = min(256, width)
    total = sum(right.shape[1] for _, right in pairs)
    return pl.pallas_call(
        functools.partial(weight_grads_kernel, len(pairs)),
        grid=(width // tile,),
        in_specs=[pl.BlockSpec((left.shape[0], tile), lambda i: (0, i)) for left, _ in pairs]
        + [pl.BlockSpec(right.shape, lambda i: (0, 0)) for _, right in pairs],
        out_specs=pl.BlockSpec((tile, total), lambda i: (i, 0)),
        out_shape=jax.ShapeDtypeStruct((width, total), BF16),
        compiler_params=pltpu.CompilerParams(vmem_limit_bytes=40 * 2**20),
    )(*[left for left, _ in pairs], *[right for _, right in pairs])


def pack_kernel(count, which_ref, *refs):
    mine_ref, other_ref = refs[count:]
    for mine in range(2):

        @pl.when(which_ref[0] == mine)
        def _():
            start = 0
            for ref in refs[:count]:
                size = ref.shape[2] // 2
                for k in range(ref.shape[0]):
                    piece = ref[k]
                    for out_ref, index in ((mine_ref, mine), (other_ref, 1 - mine)):
                        out_ref[:, start : start + size] = piece[:, index * size : (index + 1) * size]
                    start += size


def pack(which, weights):
    rows = weights[0].shape[1]
    total = sum(weight.shape[0] * (weight.shape[2] // 2) for weight in weights)
    shape = jax.ShapeDtypeStruct((rows, total), BF16)
    return pl.pallas_call(
        functools.partial(pack_kernel, len(weights)),
        in_specs=[pl.BlockSpec(memory_space=pltpu.SMEM)]
        + [pl.BlockSpec(memory_space=pltpu.VMEM)] * len(weights),
        out_specs=[pl.BlockSpec(memory_space=pltpu.VMEM)] * 2,
        out_shape=[shape, shape],
    )(which, *weights)


def assemble_kernel(count, places_ref, *refs):
    out_ref = refs[count]
    rows = refs[0].shape[0]
    for i in range(count):
        out_ref[pl.ds(pl.multiple_of(places_ref[i] * rows, rows), rows), :] = refs[i][...]


def assemble(places, pieces):
    rows, columns = pieces[0].shape
    return pl.pallas_call(
        functools.partial(assemble_kernel, len(pieces)),
        in_specs=[pl.BlockSpec(memory_space=pltpu.SMEM)]
        + [pl.BlockSpec(memory_space=pltpu.VMEM)] * len(pieces),
        out_specs=pl.BlockSpec(memory_space=pltpu.VMEM),
        out_shape=jax.ShapeDtypeStruct((rows * len(pieces), columns), BF16),
        compiler_params=pltpu.CompilerParams(vmem_limit_bytes=40 * 2**20),
    )(places, *pieces)


def layer_norm(values, scales, shifts):
    row_mean = jnp.mean(values, axis=-1, keepdims=True)
    centred = values - row_mean
    variance = jnp.mean(centred * centred, axis=-1, keepdims=True)
    inverse = lax.rsqrt(variance + 1e-05)
    hat = centred * inverse
    return hat * scales + shifts, hat, inverse


def norm_back(hat, inverse, scales, incoming):
    scaled = incoming * scales
    return (
        scaled
        - jnp.mean(scaled, axis=-1, keepdims=True)
        - hat * jnp.mean(scaled * hat, axis=-1, keepdims=True)
    ) * inverse


def build(fsdp, ctx, tp):
    assert ctx == 2
    ring = list(range(0, fsdp, 2)) + list(range(fsdp - 1, 0, -2)) if fsdp > 1 else [0]
    onward = [(ring[i], ring[(i + 1) % fsdp]) for i in range(fsdp)]
    backward_ring = [(b, a) for a, b in onward]
    swap = [(0, 1), (1, 0)]

    def ring_place(index):
        return jnp.where(index % 2 == 0, index // 2, fsdp - 1 - index // 2)

    def ring_index(place):
        place = place % fsdp
        return jnp.where(2 * place < fsdp, 2 * place, 2 * fsdp - 1 - 2 * place)

    def ctx_swap(values):
        return lax.ppermute(values, "ctx", swap)

    def tp_swap(values):
        return lax.ppermute(values, "tp", swap)

    def ordered(first, second, index, axis):
        return jnp.where(
            index == 0,
            jnp.concatenate((first, second), axis=axis),
            jnp.concatenate((second, first), axis=axis),
        )

    def after(values, token):
        return lax.optimization_barrier((values, token))[0]

    def per_device(
        inputs,
        encoder_states,
        self_weights,
        self_output,
        cross_query,
        cross_memory,
        cross_output,
        hidden_in,
        hidden_out,
        norm_gains,
        norm_shifts,
        head_biases,
        output_biases,
        hidden_bias,
        cotangent,
    ):
        f, c, t = lax.axis_index("fsdp"), lax.axis_index("ctx"), lax.axis_index("tp")
        place = ring_place(f)
        rows, width = inputs.shape[1], inputs.shape[2]
        part = rows // tp
        half_rows = ctx * part
        shard = self_weights.shape[0]
        q_self = self_weights.shape[2] // ctx
        q_hidden = hidden_in.shape[1] // ctx

        def all_halves(half):
            if tp == 2:
                return jnp.concatenate((half, tp_swap(half)), axis=0)
            return lax.all_gather(half, "tp", axis=0, tiled=True)

        def own_half(values):
            if tp == 2:
                return values[:half_rows]
            return lax.dynamic_slice_in_dim(values, t * half_rows, half_rows, axis=0)

        def own_part(half):
            return lax.dynamic_slice_in_dim(half, c * part, part, axis=0)

        def group_sum(partial):
            if tp == 2:
                mine = partial[:half_rows] + tp_swap(partial[half_rows:].astype(BF16)).astype(F32)
            else:
                mine = lax.psum_scatter(
                    partial.astype(BF16), "tp", scatter_dimension=0, tiled=True
                )
            mine = mine.astype(BF16)
            return mine.astype(F32) + ctx_swap(mine).astype(F32)

        def chip_rows(half):
            own = own_part(half)
            if tp == 2:
                return ordered(own, tp_swap(own), t, 0)
            return lax.all_gather(own, "tp", axis=0, tiled=True)

        def half_of(values):
            own = lax.dynamic_slice_in_dim(values, t * part, part, axis=0)
            return ordered(own, ctx_swap(own), c, 0)

        which = c.astype(jnp.int32).reshape(1)
        steps = jnp.arange(fsdp, dtype=jnp.int32)
        piece_places = jnp.stack(
            (
                ring_index(place + fsdp - steps) * ctx + c,
                ring_index(place + steps) * ctx + 1 - c,
            ),
            axis=1,
        ).reshape(-1)
        piece_places = piece_places.astype(jnp.int32)

        def ring_gather(mine, other):
            trail = [(mine, other)]
            for step in range(1, fsdp):
                mine = lax.ppermute(mine, "fsdp", onward)
                other = lax.ppermute(other, "fsdp", backward_ring)
                mine, other = lax.optimization_barrier((mine, other))
                trail.append((mine, other))
            full = assemble(piece_places, [piece for pair in trail for piece in pair])
            return full, trail

        def offload_scatter(gradients):
            blocks = gradients.reshape(fsdp, ctx, shard, -1)
            total = lax.psum_scatter(blocks, "fsdp", scatter_dimension=0, tiled=False)
            return (
                lax.dynamic_index_in_dim(total, c, 0, keepdims=False),
                lax.dynamic_index_in_dim(total, 1 - c, 0, keepdims=False),
            )

        def direct_scatter(gradients, spans):
            blocks = lax.all_to_all(
                gradients, ("fsdp", "ctx"), split_axis=0, concat_axis=0, tiled=True
            )
            blocks = blocks.reshape(fsdp, ctx, shard, -1).astype(F32)
            total, results, start = jnp.sum(blocks, axis=0), [], 0
            for count, size in spans:
                stop = start + count * size
                piece = total[:, :, start:stop].reshape(ctx, shard, count, size)
                results.append(jnp.transpose(piece, (1, 2, 0, 3)).reshape(shard, count, -1))
                start = stop
            return results

        def to_owners(scattered, spans):
            mine, theirs = scattered
            theirs = ctx_swap(theirs)
            results, start = [], 0
            for count, size in spans:
                stop = start + count * size
                a = mine[:, start:stop].reshape(shard, count, 1, size)
                b = theirs[:, start:stop].reshape(shard, count, 1, size)
                results.append(ordered(a, b, c, 2).reshape(shard, count, -1).astype(F32))
                start = stop
            return results

        mine, other = pack(
            which,
            [
                jnp.transpose(self_weights, (1, 0, 2)),
                jnp.transpose(cross_memory, (1, 0, 2)),
                self_output.T[None],
                cross_query[None],
                cross_output.T[None],
            ],
        )
        other = ctx_swap(other)
        w_attention, trail = ring_gather(mine, other)
        token_half = half_of(after(inputs[0], trail[1]))
        frames_here = after(encoder_states[0], trail[2])
        mine, other = pack(which, [hidden_in[None], hidden_out.T[None]])
        other = ctx_swap(other)
        w_hidden = lax.all_gather(ordered(mine, other, c, 0), "fsdp", axis=0, tiled=True)
        cot_here = after(cotangent[0], trail[-2])
        w_qkv, w_mid = w_attention[:, : 3 * q_self], w_attention[:, 3 * q_self :]
        w_memory = w_mid[:, : 2 * q_self]
        w_self_out = w_mid[:, 2 * q_self : 3 * q_self]
        w_query = w_mid[:, 3 * q_self : 4 * q_self]
        w_cross_out = w_mid[:, 4 * q_self :]
        w_in, w_out = w_hidden[:, :q_hidden], w_hidden[:, q_hidden:]

        def my_bias(bias):
            return lax.dynamic_index_in_dim(
                bias.reshape(bias.shape[:-1] + (ctx, -1)), c, bias.ndim - 1, keepdims=False
            )

        head_bias = my_bias(head_biases)
        hidden_own_bias = my_bias(hidden_bias)

        tokens = all_halves(token_half).astype(F32)
        frame_rows = frames_here.shape[0]
        frame_half = -(-frame_rows // 256) * 256
        piece = ctx_swap(
            lax.dynamic_slice_in_dim(frames_here, t * (width // tp), width // tp, axis=1)
        )
        if tp == 2:
            frames_there = ordered(piece, tp_swap(piece), t, 1)
        else:
            frames_there = lax.all_gather(piece, "tp", axis=1, tiled=True)
        blank = ((0, frame_half - frame_rows), (0, 0))
        frames = jnp.concatenate((jnp.pad(frames_here, blank), jnp.pad(frames_there, blank)), axis=0)
        cot_half = half_of(cot_here)
        cot_all = all_halves(cot_half)
        stream_half = own_half(tokens)

        normed_one, hat_one, inverse_one = layer_norm(tokens, norm_gains[0], norm_shifts[0])
        normed_one = normed_one.astype(BF16)
        projected = mm(normed_one, w_qkv, 1, 0)
        queries = (projected[:, :q_self] + head_bias[0]).astype(BF16)
        self_keys = projected[:, q_self : 2 * q_self].astype(BF16)
        self_values = (projected[:, 2 * q_self :] + head_bias[1]).astype(BF16)
        j = jnp.arange(ctx * rows, dtype=jnp.int32)
        jt, jc, i = j // half_rows, (j // part) % ctx, j % part
        if tp == 2:
            jt = jt ^ t
        position = jc * rows + jt * part + i
        places = (position[:, None], position[None, :])
        self_mixed, self_exact, self_totals = attend_forward(
            queries, self_keys, self_values, ctx * rows, ctx * rows, places
        )
        after_self = stream_half + (group_sum(mm(self_mixed, w_self_out, 1, 1)) + output_biases[0])
        normed_two, hat_two, inverse_two = layer_norm(after_self, norm_gains[1], norm_shifts[1])
        normed_two = all_halves(normed_two.astype(BF16))
        cross_queries = (mm(normed_two, w_query, 1, 0) + head_bias[2]).astype(BF16)
        memory_bias = jnp.concatenate((jnp.zeros((q_self,), F32), head_bias[3]))
        frame_proj = (mm(frames, w_memory, 1, 0) + memory_bias).astype(BF16)
        frame_keys, frame_values = frame_proj[:, :q_self], frame_proj[:, q_self:]
        cross_mixed, cross_exact, cross_totals = attend_forward(
            cross_queries, frame_keys, frame_values, frame_rows, frame_half
        )
        after_cross = after_self + (
            group_sum(mm(cross_mixed, w_cross_out, 1, 1)) + output_biases[1]
        )
        normed_three, hat_three, inverse_three = layer_norm(
            after_cross, norm_gains[2], norm_shifts[2]
        )
        normed_three = all_halves(normed_three.astype(BF16))
        pre_gelu = mm(normed_three, w_in, 1, 0) + hidden_own_bias
        cdf = 0.5 * (1.0 + lax.erf(pre_gelu * (0.5**0.5)))
        activated = (pre_gelu * cdf).astype(BF16)
        slope = cdf + pre_gelu * jnp.exp(-0.5 * pre_gelu * pre_gelu) * 0.3989422804014327

        grad_pre = (mm(cot_all, w_out, 1, 0) * slope).astype(BF16)
        grad_three = group_sum(mm(grad_pre, w_in, 1, 1))
        hidden_total = group_sum(mm(activated, w_out, 1, 1))
        output_half = (after_cross + (hidden_total + output_biases[2])).astype(BF16)
        layer_output = chip_rows(output_half)[None]
        grad_hidden = weight_grads([(normed_three, grad_pre), (cot_all, activated)])
        hidden_scattered = offload_scatter(grad_hidden)
        grad_three = after(grad_three, grad_hidden)
        grad_after_cross = cot_half.astype(F32) + norm_back(
            hat_three, inverse_three, norm_gains[2], grad_three
        )
        grad_cross_half = grad_after_cross.astype(BF16)
        grad_cross = all_halves(grad_cross_half)

        grad_cross_mixed = mm(grad_cross, w_cross_out, 1, 0).astype(BF16)
        grad_cross_queries, grad_fkeys, grad_fvalues = attend_backward(
            cross_queries,
            frame_keys,
            frame_values,
            grad_cross_mixed,
            cross_exact,
            cross_totals,
            frame_rows,
            frame_half,
        )
        grad_two = group_sum(mm(grad_cross_queries, w_query, 1, 1))
        grad_frames = jnp.concatenate((grad_fkeys, grad_fvalues), axis=1)
        grad_attention = weight_grads(
            [(frames, grad_frames), (grad_cross, cross_mixed), (normed_two, grad_cross_queries)]
        )
        grad_two = after(grad_two, grad_attention)
        grad_memory, grad_cross_output, grad_cross_query = direct_scatter(
            grad_attention, [(2, q_self), (1, q_self), (1, q_self)]
        )
        encoder_part = mm(grad_frames, w_memory, 1, 1).astype(BF16)
        if tp == 2:
            half = width // 2
            keep = lax.dynamic_slice_in_dim(encoder_part, t * half, half, axis=1)
            give = lax.dynamic_slice_in_dim(encoder_part, (1 - t) * half, half, axis=1)
            encoder_sum = (keep.astype(F32) + tp_swap(give).astype(F32)).astype(BF16)
        else:
            encoder_sum = lax.psum_scatter(
                encoder_part, "tp", scatter_dimension=1, tiled=True
            )
        grad_encoder = (
            encoder_sum[:frame_rows].astype(F32)
            + ctx_swap(encoder_sum[frame_half : frame_half + frame_rows]).astype(F32)
        )[None]

        grad_after_self = grad_after_cross + norm_back(
            hat_two, inverse_two, norm_gains[1], grad_two
        )
        grad_self_half = grad_after_self.astype(BF16)
        grad_self = all_halves(grad_self_half)

        grad_self_mixed = mm(grad_self, w_self_out, 1, 0).astype(BF16)
        grad_queries, grad_keys, grad_values = attend_backward(
            queries,
            self_keys,
            self_values,
            grad_self_mixed,
            self_exact,
            self_totals,
            ctx * rows,
            ctx * rows,
            places,
        )
        grad_projected = jnp.concatenate((grad_queries, grad_keys, grad_values), axis=1)
        grad_self_weights, grad_self_output = direct_scatter(
            weight_grads([(normed_one, grad_projected), (grad_self, self_mixed)]),
            [(3, q_self), (1, q_self)],
        )
        grad_one = group_sum(mm(grad_projected, w_qkv, 1, 1))
        hat_one, inverse_one = own_half(hat_one), own_half(inverse_one)
        grad_inputs = chip_rows(
            grad_after_self + norm_back(hat_one, inverse_one, norm_gains[0], grad_one)
        )[None]

        grad_hidden_in, grad_hidden_out = to_owners(
            hidden_scattered, [(1, q_hidden), (1, q_hidden)]
        )

        def column_sum(values):
            return jnp.sum(values.astype(F32), axis=0)

        wide = jnp.stack(
            (
                column_sum(grad_one * hat_one),
                column_sum(hat_two * grad_two),
                column_sum(hat_three * grad_three),
                column_sum(grad_one),
                column_sum(grad_two),
                column_sum(grad_three),
                column_sum(grad_self_half),
                column_sum(grad_cross_half),
                column_sum(cot_half),
            )
        )
        narrow = jnp.concatenate(
            (
                column_sum(grad_queries),
                column_sum(grad_values),
                column_sum(grad_cross_queries),
                column_sum(grad_fvalues),
                column_sum(grad_pre),
            )
        )
        if tp == 2:
            wide = wide + tp_swap(wide)
        else:
            wide = lax.psum(wide, "tp")
        small = jnp.concatenate((wide.reshape(-1), narrow))
        hop = 1
        while hop < fsdp:
            small = small + lax.ppermute(small, "fsdp", [(i, i ^ hop) for i in range(fsdp)])
            hop *= 2
        wide = small[: 9 * width].reshape(9, width)
        narrow = small[9 * width :]
        both = ordered(narrow[None], ctx_swap(narrow)[None], c, 0)
        grad_head = both[:, : 4 * q_self].reshape(ctx, 4, q_self)
        grad_head = jnp.transpose(grad_head, (1, 0, 2)).reshape(4, -1)
        grad_hidden_bias = both[:, 4 * q_self :].reshape(-1)
        return (
            layer_output,
            grad_inputs,
            grad_encoder,
            grad_self_weights,
            grad_self_output[:, 0].T,
            grad_cross_query[:, 0],
            grad_memory,
            grad_cross_output[:, 0].T,
            grad_hidden_in[:, 0],
            grad_hidden_out[:, 0].T,
            wide[0:3],
            wide[3:6],
            grad_head,
            wide[6:9],
            grad_hidden_bias,
        )

    return per_device


def solution(mesh):
    in_specs = (
        P("fsdp", "ctx", None),
        P("fsdp", "ctx", None),
        P(("fsdp", "ctx"), None, "tp"),
        P("tp", ("fsdp", "ctx")),
        P(("fsdp", "ctx"), "tp"),
        P(("fsdp", "ctx"), None, "tp"),
        P("tp", ("fsdp", "ctx")),
        P(("fsdp", "ctx"), "tp"),
        P("tp", ("fsdp", "ctx")),
        P(),
        P(),
        P(None, "tp"),
        P(),
        P("tp"),
        P("fsdp", "ctx", None),
    )
    out_specs = (
        P("fsdp", "ctx", None),
        P("fsdp", "ctx", None),
        P("fsdp", "ctx", "tp"),
        P(("fsdp", "ctx"), None, "tp"),
        P("tp", ("fsdp", "ctx")),
        P(("fsdp", "ctx"), "tp"),
        P(("fsdp", "ctx"), None, "tp"),
        P("tp", ("fsdp", "ctx")),
        P(("fsdp", "ctx"), "tp"),
        P("tp", ("fsdp", "ctx")),
        P(),
        P(),
        P(None, "tp"),
        P(),
        P("tp"),
    )
    per_device = build(mesh.shape["fsdp"], mesh.shape["ctx"], mesh.shape["tp"])
    return jax.shard_map(
        per_device, mesh=mesh, in_specs=in_specs, out_specs=out_specs, check_vma=False
    )
```

```python
import functools

import jax
import jax.numpy as jnp
from jax import lax
from jax.experimental import pallas as pl
from jax.experimental.pallas import tpu as pltpu
from jax.sharding import PartitionSpec as P

HEAD_DIM = 64
SCALING = HEAD_DIM ** (-0.5)
F32 = jnp.float32
BF16 = jnp.bfloat16


def key_tile(total):
    return 256 if total % 256 == 0 else total

def mm(left, right, left_dim, right_dim):
    return lax.dot_general(
        left, right, (((left_dim,), (right_dim,)), ((), ())), preferred_element_type=F32
    )

def only_head(values, head, group):
    if group == HEAD_DIM: return values
    lane = lax.broadcasted_iota(jnp.int32, values.shape, 1)
    return jnp.where(lane // HEAD_DIM == head, values, jnp.zeros_like(values))

def visible(tile, queries, start, used, half, key_place, query_place):
    if key_place is not None:
        return key_place[start:start+tile, :] <= query_place[...]
    row = start % half
    if row + tile > used:
        return row + lax.broadcasted_iota(jnp.int32, (tile, queries), 0) < used
    return None

def forward_kernel(used, half, causal, *refs):
    if causal:
        kp, qp, q_ref, k_ref, v_ref, mixed_ref, exact_ref, totals_ref = refs
    else:
        q_ref, k_ref, v_ref, mixed_ref, exact_ref, totals_ref = refs; kp = qp = None
    keys, group = k_ref.shape; queries = q_ref.shape[0]; tile = key_tile(keys)
    heads = group // HEAD_DIM
    q = (q_ref[...].astype(F32) * SCALING).astype(BF16)
    starts = range(0, keys, tile)
    qs = [only_head(q, h, group) for h in range(heads)]
    scores = [[None] * len(starts) for _ in range(heads)]
    tops = [None] * heads
    for i, start in enumerate(starts):
        ok = visible(tile, queries, start, used, half, kp, qp)
        for h in range(heads):
            s = mm(k_ref[start:start+tile, :], qs[h], 1, 1)
            if ok is not None: s = jnp.where(ok, s, -1e30)
            m = jnp.max(s, axis=0, keepdims=True)
            tops[h] = m if tops[h] is None else jnp.maximum(tops[h], m)
            scores[h][i] = s
    totals = [None] * heads; accs = [None] * heads
    for i, start in enumerate(starts):
        for h in range(heads):
            e = jnp.exp(scores[h][i] - tops[h])
            es = jnp.sum(e, axis=0, keepdims=True)
            o = mm(v_ref[start:start+tile, :], e.astype(BF16), 0, 0)
            totals[h] = es if totals[h] is None else totals[h] + es
            accs[h] = o if accs[h] is None else accs[h] + o
    for h in range(heads):
        rows = slice(h*HEAD_DIM, (h+1)*HEAD_DIM)
        exact_ref[rows, :] = accs[h][rows, :] * (1.0/totals[h])
        totals_ref[0, h:h+1, :] = tops[h] + jnp.log(totals[h])
    mixed_ref[...] = exact_ref[...].T.astype(BF16)

def backward_kernel(used, half, causal, *refs):
    if causal:
        kp, qp, q_ref, k_ref, v_ref, g_ref, exact_ref, totals_ref, dq_ref, dk_ref, dv_ref = refs
    else:
        q_ref, k_ref, v_ref, g_ref, exact_ref, totals_ref, dq_ref, dk_ref, dv_ref = refs; kp = qp = None
    keys, group = k_ref.shape; queries = q_ref.shape[0]; tile = key_tile(keys)
    heads = group // HEAD_DIM
    q = (q_ref[...].astype(F32) * SCALING).astype(BF16)
    g = g_ref[...]
    both = exact_ref[...] * g.astype(F32).T
    qs = [only_head(q, h, group) for h in range(heads)]
    gs = [only_head(g, h, group) for h in range(heads)]
    dots = [jnp.sum(both[h*HEAD_DIM:(h+1)*HEAD_DIM, :], axis=0, keepdims=True) for h in range(heads)]
    dqs = [None]*heads
    for start in range(0, keys, tile):
        k = k_ref[start:start+tile, :]; v = v_ref[start:start+tile, :]
        ok = visible(tile, queries, start, used, half, kp, qp)
        dk = dv = None
        for h in range(heads):
            s = mm(k, qs[h], 1, 1)
            if ok is not None: s = jnp.where(ok, s, -1e30)
            p = jnp.exp(s - totals_ref[0, h:h+1, :])
            dp = mm(v, gs[h], 1, 1)
            ds = (p * (dp - dots[h])).astype(BF16)
            a = mm(ds, qs[h], 1, 0); b = mm(p.astype(BF16), gs[h], 1, 0)
            dk = a if dk is None else dk + a
            dv = b if dv is None else dv + b
            c = mm(k, ds, 0, 0)
            dqs[h] = c if dqs[h] is None else dqs[h] + c
        dk_ref[start:start+tile, :] = dk.astype(BF16)
        dv_ref[start:start+tile, :] = dv.astype(BF16)
    full = jnp.concatenate([dqs[h][h*HEAD_DIM:(h+1)*HEAD_DIM, :] for h in range(heads)], axis=0)
    dq_ref[...] = (full.T * SCALING).astype(BF16)

def attend_forward(q, k, v, used, half, places=None):
    queries, width = q.shape; keys = k.shape[0]; group = min(128, width); n = width//group
    col = lambda rows: pl.BlockSpec((rows, group), lambda i: (0, i))
    fixed = lambda shape: pl.BlockSpec(shape, lambda i: (0, 0))
    extra = [] if places is None else list(places)
    return pl.pallas_call(
        functools.partial(forward_kernel, used, half, places is not None),
        grid=(n,),
        in_specs=[fixed(p.shape) for p in extra]+[col(queries), col(keys), col(keys)],
        out_specs=[col(queries), pl.BlockSpec((group, queries), lambda i: (i, 0)), pl.BlockSpec((1, group//HEAD_DIM, queries), lambda i: (i,0,0))],
        out_shape=[jax.ShapeDtypeStruct((queries,width),BF16), jax.ShapeDtypeStruct((width,queries),F32), jax.ShapeDtypeStruct((n,group//HEAD_DIM,queries),F32)],
        compiler_params=pltpu.CompilerParams(vmem_limit_bytes=20 * 2**20),
    )(*extra, q, k, v)

def attend_backward(q, k, v, g, exact, totals, used, half, places=None):
    queries, width = q.shape; keys = k.shape[0]; group = min(128, width); n = width//group
    col = lambda rows: pl.BlockSpec((rows, group), lambda i: (0, i))
    fixed = lambda shape: pl.BlockSpec(shape, lambda i: (0, 0))
    extra = [] if places is None else list(places)
    return pl.pallas_call(
        functools.partial(backward_kernel, used, half, places is not None),
        grid=(n,),
        in_specs=[fixed(p.shape) for p in extra]+[col(queries), col(keys), col(keys), col(queries), pl.BlockSpec((group, queries), lambda i: (i, 0)), pl.BlockSpec((1, group//HEAD_DIM, queries), lambda i: (i,0,0))],
        out_specs=[col(queries), col(keys), col(keys)],
        out_shape=[jax.ShapeDtypeStruct((queries,width),BF16), jax.ShapeDtypeStruct((keys,width),BF16), jax.ShapeDtypeStruct((keys,width),BF16)],
        compiler_params=pltpu.CompilerParams(vmem_limit_bytes=20 * 2**20),
    )(*extra, q, k, v, g, exact, totals)


def weight_grads_kernel(count, order_ref, which_ref, *refs):
    out_ref, start = refs[2 * count], 0
    rows = out_ref.shape[2]
    step = pl.program_id(0)
    for i in range(count):
        left, right = refs[i], refs[count + i]
        stop = start + right.shape[1]
        total = mm(left[...], right[...], 0, 0).astype(BF16)
        devices = total.shape[0] // (2 * rows)
        for j in range(devices):
            place = order_ref[step * devices + j]
            for half in range(2):
                row = (2 * j + half) * rows
                out_ref[place, (which_ref[0] == half).astype(jnp.int32), :, start:stop] = total[
                    row : row + rows, :
                ]
        start = stop


def weight_grads(order, which, pairs):
    steps, width = order.shape[0], pairs[0][0].shape[1]
    rows, total = width // steps, sum(right.shape[1] for _, right in pairs)
    count, tile = len(pairs), max(256, rows)
    out = (steps, 2, rows // 2, total)
    return pl.pallas_call(
        functools.partial(weight_grads_kernel, count),
        grid_spec=pltpu.PrefetchScalarGridSpec(
            num_scalar_prefetch=2,
            grid=(width // tile,),
            in_specs=[
                pl.BlockSpec((left.shape[0], tile), lambda i, order, which: (0, i))
                for left, _ in pairs
            ]
            + [pl.BlockSpec(right.shape, lambda i, order, which: (0, 0)) for _, right in pairs],
            out_specs=pl.BlockSpec(out, lambda i, order, which: (0, 0, 0, 0)),
        ),
        out_shape=jax.ShapeDtypeStruct(out, BF16),
        compiler_params=pltpu.CompilerParams(vmem_limit_bytes=20 * 2**20),
    )(order, which, *[left for left, _ in pairs], *[right for _, right in pairs])


def ring_add_kernel(counts, *refs):
    ins, outs = refs[: len(refs) - len(counts)], refs[len(refs) - len(counts) :]
    at = 0
    for count, out_ref in zip(counts, outs):
        moved, start = ins[at], 0
        for part in ins[at + 1 : at + 1 + count]:
            stop = start + part.shape[1]
            total = moved[:, start:stop].astype(F32) + part[...].astype(F32)
            out_ref[:, start:stop] = total.astype(BF16)
            start = stop
        at += 1 + count


def ring_add(items):
    specs, operands = [], []
    for moved, parts, distance, half in items:
        specs.append(pl.BlockSpec(memory_space=pltpu.VMEM))
        operands.append(moved)
        for part in parts:
            block = (None, None) + part.shape[2:]
            specs.append(pl.BlockSpec(block, lambda i, d=distance, h=half: (d, h, 0, 0)))
            operands.append(part)
    return pl.pallas_call(
        functools.partial(ring_add_kernel, [len(parts) for _, parts, _, _ in items]),
        grid=(1,),
        in_specs=specs,
        out_specs=[pl.BlockSpec(memory_space=pltpu.VMEM)] * len(items),
        out_shape=[jax.ShapeDtypeStruct(moved.shape, BF16) for moved, _, _, _ in items],
        compiler_params=pltpu.CompilerParams(vmem_limit_bytes=6 * 2**20),
    )(*operands)


def pack_kernel(count, which_ref, *refs):
    mine_ref, other_ref = refs[count:]
    for mine in range(2):

        @pl.when(which_ref[0] == mine)
        def _():
            start = 0
            for ref in refs[:count]:
                size = ref.shape[2] // 2
                for k in range(ref.shape[0]):
                    piece = ref[k]
                    for out_ref, index in ((mine_ref, mine), (other_ref, 1 - mine)):
                        out_ref[:, start : start + size] = piece[:, index * size : (index + 1) * size]
                    start += size


def pack(which, weights):
    rows = weights[0].shape[1]
    total = sum(weight.shape[0] * (weight.shape[2] // 2) for weight in weights)
    shape = jax.ShapeDtypeStruct((rows, total), BF16)
    return pl.pallas_call(
        functools.partial(pack_kernel, len(weights)),
        in_specs=[pl.BlockSpec(memory_space=pltpu.SMEM)]
        + [pl.BlockSpec(memory_space=pltpu.VMEM)] * len(weights),
        out_specs=[pl.BlockSpec(memory_space=pltpu.VMEM)] * 2,
        out_shape=[shape, shape],
        compiler_params=pltpu.CompilerParams(vmem_limit_bytes=6 * 2**20),
    )(which, *weights)


def unpack_kernel(counts, which_ref, mine_ref, theirs_ref, *out_refs):
    for mine in range(2):

        @pl.when(which_ref[0] == mine)
        def _():
            start = 0
            for ref, count in zip(out_refs, counts):
                size = ref.shape[2] // 2
                for k in range(count):
                    for in_ref, index in ((mine_ref, mine), (theirs_ref, 1 - mine)):
                        ref[k, :, index * size : (index + 1) * size] = in_ref[
                            :, start : start + size
                        ].astype(F32)
                    start += size


def unpack(which, mine, theirs, spans):
    rows = mine.shape[0]
    return pl.pallas_call(
        functools.partial(unpack_kernel, [count for count, _ in spans]),
        in_specs=[pl.BlockSpec(memory_space=pltpu.SMEM)]
        + [pl.BlockSpec(memory_space=pltpu.VMEM)] * 2,
        out_specs=[pl.BlockSpec(memory_space=pltpu.VMEM)] * len(spans),
        out_shape=[jax.ShapeDtypeStruct((count, rows, 2 * size), F32) for count, size in spans],
        compiler_params=pltpu.CompilerParams(vmem_limit_bytes=6 * 2**20),
    )(which, mine, theirs)


def assemble_kernel(count, places_ref, *refs):
    out_ref, sems = refs[count], refs[count + 1]
    rows = refs[0].shape[0]

    def copy(i):
        start = pl.multiple_of(places_ref[i] * rows, rows)
        return pltpu.make_async_copy(refs[i], out_ref.at[pl.ds(start, rows), :], sems.at[i])

    for i in range(count):
        copy(i).start()
    for i in range(count):
        copy(i).wait()


def assemble(places, pieces):
    rows, columns = pieces[0].shape
    return pl.pallas_call(
        functools.partial(assemble_kernel, len(pieces)),
        in_specs=[pl.BlockSpec(memory_space=pltpu.SMEM)]
        + [pl.BlockSpec(memory_space=pl.ANY)] * len(pieces),
        out_specs=pl.BlockSpec(memory_space=pltpu.VMEM),
        out_shape=jax.ShapeDtypeStruct((rows * len(pieces), columns), BF16),
        scratch_shapes=[pltpu.SemaphoreType.DMA((len(pieces),))],
        compiler_params=pltpu.CompilerParams(vmem_limit_bytes=16 * 2**20),
    )(places, *pieces)


def layer_norm(values, scales, shifts):
    row_mean = jnp.mean(values, axis=-1, keepdims=True)
    centred = values - row_mean
    variance = jnp.mean(centred * centred, axis=-1, keepdims=True)
    inverse = lax.rsqrt(variance + 1e-05)
    hat = centred * inverse
    return hat * scales + shifts, hat, inverse


def norm_back(hat, inverse, scales, incoming):
    scaled = incoming * scales
    return (
        scaled
        - jnp.mean(scaled, axis=-1, keepdims=True)
        - hat * jnp.mean(scaled * hat, axis=-1, keepdims=True)
    ) * inverse


def advance(rider, value):
    try:
        return [(rider,) + rider.send(value)]
    except StopIteration:
        return []


def build(fsdp, ctx, tp):
    assert ctx == 2
    ring = list(range(0, fsdp, 2)) + list(range(fsdp - 1, 0, -2)) if fsdp > 1 else [0]
    onward = [(ring[i], ring[(i + 1) % fsdp]) for i in range(fsdp)]
    backward_ring = [(b, a) for a, b in onward]
    swap = [(0, 1), (1, 0)]

    def ring_place(index):
        return jnp.where(index % 2 == 0, index // 2, fsdp - 1 - index // 2)

    def ring_index(place):
        place = place % fsdp
        return jnp.where(2 * place < fsdp, 2 * place, 2 * fsdp - 1 - 2 * place)

    def ctx_swap(values):
        return lax.ppermute(values, "ctx", swap)

    def tp_swap(values):
        return lax.ppermute(values, "tp", swap)

    def ordered(first, second, index, axis):
        return jnp.where(
            index == 0,
            jnp.concatenate((first, second), axis=axis),
            jnp.concatenate((second, first), axis=axis),
        )

    def after(values, token):
        return lax.optimization_barrier((values, token))[0]

    def per_device(
        inputs,
        encoder_states,
        self_weights,
        self_output,
        cross_query,
        cross_memory,
        cross_output,
        hidden_in,
        hidden_out,
        norm_gains,
        norm_shifts,
        head_biases,
        output_biases,
        hidden_bias,
        cotangent,
    ):
        f, c, t = lax.axis_index("fsdp"), lax.axis_index("ctx"), lax.axis_index("tp")
        place = ring_place(f)
        rows, width = inputs.shape[1], inputs.shape[2]
        part = rows // tp
        half_rows = ctx * part
        shard = self_weights.shape[0]
        q_self = self_weights.shape[2] // ctx
        q_hidden = hidden_in.shape[1] // ctx

        def all_halves(half):
            if tp == 2:
                return jnp.concatenate((half, tp_swap(half)), axis=0)
            return lax.all_gather(half, "tp", axis=0, tiled=True)

        def own_half(values):
            if tp == 2:
                return values[:half_rows]
            return lax.dynamic_slice_in_dim(values, t * half_rows, half_rows, axis=0)

        def own_part(half):
            return lax.dynamic_slice_in_dim(half, c * part, part, axis=0)

        def group_sum(partial, hook=lambda mine: mine):
            if tp == 2:
                mine = partial[:half_rows] + tp_swap(partial[half_rows:].astype(BF16)).astype(F32)
            else:
                mine = lax.psum_scatter(
                    partial.astype(BF16), "tp", scatter_dimension=0, tiled=True
                )
            mine = hook(mine.astype(BF16))
            return mine.astype(F32) + ctx_swap(mine).astype(F32)

        def chip_rows(half):
            own = own_part(half)
            if tp == 2:
                return ordered(own, tp_swap(own), t, 0)
            return lax.all_gather(own, "tp", axis=0, tiled=True)

        def half_of(values):
            own = lax.dynamic_slice_in_dim(values, t * part, part, axis=0)
            return ordered(own, ctx_swap(own), c, 0)

        which = c.astype(jnp.int32).reshape(1)
        steps = jnp.arange(fsdp, dtype=jnp.int32)
        piece_places = jnp.stack(
            (
                ring_index(place + fsdp - steps) * ctx + c,
                ring_index(place + steps) * ctx + 1 - c,
            ),
            axis=1,
        ).reshape(-1)
        piece_places = piece_places.astype(jnp.int32)

        ring_order = ((ring_place(steps) - place) % fsdp).astype(jnp.int32)

        class GatherRing:
            def __init__(self, mine, other):
                self.trail = [(mine, other)]

            def turn(self, values=()):
                mine, other = self.trail[-1]
                mine = lax.ppermute(mine, "fsdp", onward)
                other = lax.ppermute(other, "fsdp", backward_ring)
                mine, other, values = lax.optimization_barrier((mine, other, values))
                self.trail.append((mine, other))
                return values

            def finish(self):
                while len(self.trail) < fsdp:
                    self.turn()
                return assemble(piece_places, [piece for pair in self.trail for piece in pair])

        class ScatterRing:
            def __init__(self, parts):
                self.parts = parts
                self.theirs = self.block(fsdp - 1, 0)
                self.mine = self.block(1 % fsdp, 1)
                self.step = 1

            def block(self, distance, half):
                return jnp.concatenate([part[distance, half] for part in self.parts], axis=1)

            def send(self):
                return (
                    lax.ppermute(self.theirs, "fsdp", onward),
                    lax.ppermute(self.mine, "fsdp", backward_ring),
                )

            def add(self, moved):
                theirs, mine = moved
                more = self.block(fsdp - 1 - self.step, 0)
                self.theirs = (theirs.astype(F32) + more.astype(F32)).astype(BF16)
                more = self.block((1 + self.step) % fsdp, 1)
                self.mine = (mine.astype(F32) + more.astype(F32)).astype(BF16)
                self.step += 1

        def turn(rings, values):
            rings = [ring for ring in rings if ring.step < fsdp]
            moved, values = lax.optimization_barrier(([ring.send() for ring in rings], values))
            for ring, pair in zip(rings, moved):
                ring.add(pair)
            return values

        def finish(rings, riders):
            waiting = [(rider,) + next(rider) for rider in riders]
            while waiting or any(ring.step < fsdp for ring in rings):
                due = [item for item in waiting if item[2] <= 1]
                moved = turn(rings, [value for _, value, _ in due])
                waiting = [
                    (rider, value, left - 1) for rider, value, left in waiting if left > 1
                ] + [sent for item, value in zip(due, moved) for sent in advance(item[0], value)]

        mine, other = pack(
            which,
            [
                jnp.transpose(self_weights, (1, 0, 2)),
                jnp.transpose(cross_memory, (1, 0, 2)),
                self_output.T[None],
                cross_query[None],
                cross_output.T[None],
            ],
        )
        other = ctx_swap(other)
        ring = GatherRing(mine, other)
        w_attention, trail = ring.finish(), ring.trail
        token_half = half_of(after(inputs[0], trail[1]))
        frames_here = after(encoder_states[0], trail[2])
        mine, other = pack(which, [hidden_in[None], hidden_out.T[None]])
        other = ctx_swap(after(other, trail[1]))
        hidden_ring = GatherRing(*after((mine, other), trail[fsdp - 2]))
        cot_here = after(cotangent[0], trail[-2])
        w_qkv, w_mid = w_attention[:, : 3 * q_self], w_attention[:, 3 * q_self :]
        w_memory = w_mid[:, : 2 * q_self]
        w_self_out = w_mid[:, 2 * q_self : 3 * q_self]
        w_query = w_mid[:, 3 * q_self : 4 * q_self]
        w_cross_out = w_mid[:, 4 * q_self :]

        def my_bias(bias):
            return lax.dynamic_index_in_dim(
                bias.reshape(bias.shape[:-1] + (ctx, -1)), c, bias.ndim - 1, keepdims=False
            )

        head_bias = my_bias(head_biases)
        hidden_own_bias = my_bias(hidden_bias)

        tokens = all_halves(token_half).astype(F32)
        frame_rows = frames_here.shape[0]
        frame_half = -(-frame_rows // 256) * 256
        piece = ctx_swap(
            lax.dynamic_slice_in_dim(frames_here, t * (width // tp), width // tp, axis=1)
        )
        if tp == 2:
            frames_there = ordered(piece, tp_swap(piece), t, 1)
        else:
            frames_there = lax.all_gather(piece, "tp", axis=1, tiled=True)
        blank = ((0, frame_half - frame_rows), (0, 0))
        frames = jnp.concatenate((jnp.pad(frames_here, blank), jnp.pad(frames_there, blank)), axis=0)
        cot_half = half_of(cot_here)
        cot_all = all_halves(cot_half)
        stream_half = own_half(tokens)

        normed_one, hat_one, inverse_one = layer_norm(tokens, norm_gains[0], norm_shifts[0])
        normed_one = normed_one.astype(BF16)
        projected = mm(normed_one, w_qkv, 1, 0)
        (projected,) = hidden_ring.turn((projected,))
        queries = (projected[:, :q_self] + head_bias[0]).astype(BF16)
        self_keys = projected[:, q_self : 2 * q_self].astype(BF16)
        self_values = (projected[:, 2 * q_self :] + head_bias[1]).astype(BF16)
        j = jnp.arange(ctx * rows, dtype=jnp.int32)
        jt, jc, i = j // half_rows, (j // part) % ctx, j % part
        if tp == 2:
            jt = jt ^ t
        position = jc * rows + jt * part + i
        places = (position[:, None], position[None, :])
        self_mixed, self_exact, self_totals = attend_forward(
            queries, self_keys, self_values, ctx * rows, ctx * rows, places
        )
        after_self = stream_half + (
            group_sum(
                mm(self_mixed, w_self_out, 1, 1), lambda mine: hidden_ring.turn((mine,))[0]
            )
            + output_biases[0]
        )
        (after_self,) = hidden_ring.turn((after_self,))
        normed_two, hat_two, inverse_two = layer_norm(after_self, norm_gains[1], norm_shifts[1])
        normed_two = all_halves(normed_two.astype(BF16))
        cross_queries = (mm(normed_two, w_query, 1, 0) + head_bias[2]).astype(BF16)
        (cross_queries,) = hidden_ring.turn((cross_queries,))
        memory_bias = jnp.concatenate((jnp.zeros((q_self,), F32), head_bias[3]))
        frame_proj = (mm(frames, w_memory, 1, 0) + memory_bias).astype(BF16)
        frame_keys, frame_values = frame_proj[:, :q_self], frame_proj[:, q_self:]
        cross_mixed, cross_exact, cross_totals = attend_forward(
            cross_queries, frame_keys, frame_values, frame_rows, frame_half
        )
        after_cross = after_self + (
            group_sum(mm(cross_mixed, w_cross_out, 1, 1)) + output_biases[1]
        )
        normed_three, hat_three, inverse_three = layer_norm(
            after_cross, norm_gains[2], norm_shifts[2]
        )
        normed_three = all_halves(normed_three.astype(BF16))
        w_hidden = hidden_ring.finish()
        w_in, w_out = w_hidden[:, :q_hidden], w_hidden[:, q_hidden:]
        pre_gelu = mm(normed_three, w_in, 1, 0) + hidden_own_bias
        cdf = 0.5 * (1.0 + lax.erf(pre_gelu * (0.5**0.5)))
        activated = (pre_gelu * cdf).astype(BF16)
        slope = cdf + pre_gelu * jnp.exp(-0.5 * pre_gelu * pre_gelu) * 0.3989422804014327

        grad_pre = (mm(cot_all, w_out, 1, 0) * slope).astype(BF16)
        grad_three = group_sum(mm(grad_pre, w_in, 1, 1))
        hidden_total = group_sum(mm(activated, w_out, 1, 1))
        output_half = (after_cross + (hidden_total + output_biases[2])).astype(BF16)
        layer_output = chip_rows(output_half)[None]
        grad_hidden = weight_grads(ring_order, which, [(normed_three, grad_pre), (cot_all, activated)])
        hidden_ring = ScatterRing([grad_hidden])
        grad_three = after(grad_three, grad_hidden)
        grad_after_cross = cot_half.astype(F32) + norm_back(
            hat_three, inverse_three, norm_gains[2], grad_three
        )
        grad_cross_half = grad_after_cross.astype(BF16)
        grad_cross = all_halves(grad_cross_half)

        grad_cross_mixed = mm(grad_cross, w_cross_out, 1, 0).astype(BF16)
        (grad_cross_mixed,) = turn([hidden_ring], (grad_cross_mixed,))
        grad_cross_queries, grad_fkeys, grad_fvalues = attend_backward(
            cross_queries,
            frame_keys,
            frame_values,
            grad_cross_mixed,
            cross_exact,
            cross_totals,
            frame_rows,
            frame_half,
        )
        (grad_cross_queries,) = turn([hidden_ring], (grad_cross_queries,))
        grad_two = group_sum(mm(grad_cross_queries, w_query, 1, 1))
        grad_frames = jnp.concatenate((grad_fkeys, grad_fvalues), axis=1)
        cross_blocks = weight_grads(
            ring_order,
            which,
            [(frames, grad_frames), (grad_cross, cross_mixed), (normed_two, grad_cross_queries)]
        )
        (grad_two,) = turn([hidden_ring], (after(grad_two, cross_blocks),))
        grad_after_self = grad_after_cross + norm_back(
            hat_two, inverse_two, norm_gains[1], grad_two
        )
        grad_self_half = grad_after_self.astype(BF16)
        grad_self = all_halves(grad_self_half)

        grad_self_mixed = mm(grad_self, w_self_out, 1, 0).astype(BF16)
        grad_queries, grad_keys, grad_values = attend_backward(
            queries,
            self_keys,
            self_values,
            grad_self_mixed,
            self_exact,
            self_totals,
            ctx * rows,
            ctx * rows,
            places,
        )
        (grad_queries,) = turn([hidden_ring], (grad_queries,))
        grad_projected = jnp.concatenate((grad_queries, grad_keys, grad_values), axis=1)
        self_blocks = weight_grads(ring_order, which, [(normed_one, grad_projected), (grad_self, self_mixed)])
        done = {}

        def column_sum(values):
            return jnp.sum(values.astype(F32), axis=0)

        def tokens_rider():
            partial = mm(grad_projected, w_qkv, 1, 1)
            if tp == 2:
                moved = yield tp_swap(partial[half_rows:].astype(BF16)), 1
                mine = (partial[:half_rows] + moved.astype(F32)).astype(BF16)
            else:
                mine = lax.psum_scatter(
                    partial.astype(BF16), "tp", scatter_dimension=0, tiled=True
                )
            moved = yield ctx_swap(mine), 2
            grad_one = mine.astype(F32) + moved.astype(F32)
            hat, inverse = own_half(hat_one), own_half(inverse_one)
            total = own_part(grad_after_self + norm_back(hat, inverse, norm_gains[0], grad_one))
            wide = jnp.stack(
                (
                    column_sum(grad_one * hat),
                    column_sum(hat_two * grad_two),
                    column_sum(hat_three * grad_three),
                    column_sum(grad_one),
                    column_sum(grad_two),
                    column_sum(grad_three),
                    column_sum(grad_self_half),
                    column_sum(grad_cross_half),
                    column_sum(cot_half),
                )
            )
            if tp == 2:
                moved, other_rows = yield (tp_swap(wide), tp_swap(total)), 1
                wide = wide + moved
                done["inputs"] = ordered(total, other_rows, t, 0)[None]
            else:
                wide = lax.psum(wide, "tp")
                done["inputs"] = lax.all_gather(total, "tp", axis=0, tiled=True)[None]
            narrow = jnp.concatenate(
                (
                    column_sum(grad_queries),
                    column_sum(grad_values),
                    column_sum(grad_cross_queries),
                    column_sum(grad_fvalues),
                    column_sum(grad_pre),
                )
            )
            small = jnp.concatenate((wide.reshape(-1), narrow))
            hop = 1
            while hop < fsdp:
                moved = yield lax.ppermute(small, "fsdp", [(i, i ^ hop) for i in range(fsdp)]), 1
                small = small + moved
                hop *= 2
            done["wide"] = small[: 9 * width].reshape(9, width)
            narrow = small[9 * width :]
            moved = yield ctx_swap(narrow), 1
            done["narrow"] = ordered(narrow[None], moved[None], c, 0)

        def frames_rider():
            encoder_part = mm(grad_frames, w_memory, 1, 1).astype(BF16)
            if tp == 2:
                half = width // 2
                keep = lax.dynamic_slice_in_dim(encoder_part, t * half, half, axis=1)
                give = lax.dynamic_slice_in_dim(encoder_part, (1 - t) * half, half, axis=1)
                moved = yield tp_swap(give), 1
                total = (keep.astype(F32) + moved.astype(F32)).astype(BF16)
            else:
                total = lax.psum_scatter(encoder_part, "tp", scatter_dimension=1, tiled=True)
            moved = yield ctx_swap(total[frame_half : frame_half + frame_rows]), 3
            done["frames"] = (total[:frame_rows].astype(F32) + moved.astype(F32))[None]

        ring = ScatterRing([self_blocks, cross_blocks])
        finish([hidden_ring, ring], [tokens_rider(), frames_rider()])
        grad_hidden_in, grad_hidden_out = unpack(
            which,
            hidden_ring.mine,
            ctx_swap(hidden_ring.theirs),
            [(1, q_hidden), (1, q_hidden)],
        )
        (
            grad_self_weights,
            grad_self_output,
            grad_memory,
            grad_cross_output,
            grad_cross_query,
        ) = unpack(
            which,
            ring.mine,
            ctx_swap(ring.theirs),
            [(3, q_self), (1, q_self), (2, q_self), (1, q_self), (1, q_self)],
        )
        grad_inputs, grad_encoder, wide = done["inputs"], done["frames"], done["wide"]
        both = done["narrow"]
        grad_head = both[:, : 4 * q_self].reshape(ctx, 4, q_self)
        grad_head = jnp.transpose(grad_head, (1, 0, 2)).reshape(4, -1)
        grad_hidden_bias = both[:, 4 * q_self :].reshape(-1)
        return (
            layer_output,
            grad_inputs,
            grad_encoder,
            jnp.transpose(grad_self_weights, (1, 0, 2)),
            grad_self_output[0].T,
            grad_cross_query[0],
            jnp.transpose(grad_memory, (1, 0, 2)),
            grad_cross_output[0].T,
            grad_hidden_in[0],
            grad_hidden_out[0].T,
            wide[0:3],
            wide[3:6],
            grad_head,
            wide[6:9],
            grad_hidden_bias,
        )

    return per_device


def solution(mesh):
    in_specs = (
        P("fsdp", "ctx", None),
        P("fsdp", "ctx", None),
        P(("fsdp", "ctx"), None, "tp"),
        P("tp", ("fsdp", "ctx")),
        P(("fsdp", "ctx"), "tp"),
        P(("fsdp", "ctx"), None, "tp"),
        P("tp", ("fsdp", "ctx")),
        P(("fsdp", "ctx"), "tp"),
        P("tp", ("fsdp", "ctx")),
        P(),
        P(),
        P(None, "tp"),
        P(),
        P("tp"),
        P("fsdp", "ctx", None),
    )
    out_specs = (
        P("fsdp", "ctx", None),
        P("fsdp", "ctx", None),
        P("fsdp", "ctx", "tp"),
        P(("fsdp", "ctx"), None, "tp"),
        P("tp", ("fsdp", "ctx")),
        P(("fsdp", "ctx"), "tp"),
        P(("fsdp", "ctx"), None, "tp"),
        P("tp", ("fsdp", "ctx")),
        P(("fsdp", "ctx"), "tp"),
        P("tp", ("fsdp", "ctx")),
        P(),
        P(),
        P(None, "tp"),
        P(),
        P("tp"),
    )
    per_device = build(mesh.shape["fsdp"], mesh.shape["ctx"], mesh.shape["tp"])
    return jax.shard_map(
        per_device, mesh=mesh, in_specs=in_specs, out_specs=out_specs, check_vma=False
    )
```

```python
import functools

import jax
import jax.numpy as jnp
from jax import lax
from jax.experimental import pallas as pl
from jax.experimental.pallas import tpu as pltpu
from jax.sharding import PartitionSpec as P

HEAD_DIM = 64
SCALING = HEAD_DIM ** (-0.5)
F32 = jnp.float32
BF16 = jnp.bfloat16


def key_tile(total):
    return 256 if total % 256 == 0 else total

def mm(left, right, left_dim, right_dim):
    return lax.dot_general(
        left, right, (((left_dim,), (right_dim,)), ((), ())), preferred_element_type=F32
    )

def only_head(values, head, group):
    if group == HEAD_DIM: return values
    lane = lax.broadcasted_iota(jnp.int32, values.shape, 1)
    return jnp.where(lane // HEAD_DIM == head, values, jnp.zeros_like(values))

def visible(tile, queries, start, used, half, key_place, query_place):
    if key_place is not None:
        return key_place[start:start+tile, :] <= query_place[...]
    row = start % half
    if row + tile > used:
        return row + lax.broadcasted_iota(jnp.int32, (tile, queries), 0) < used
    return None

def forward_kernel(used, half, causal, *refs):
    if causal:
        kp, qp, q_ref, k_ref, v_ref, mixed_ref, exact_ref, totals_ref = refs
    else:
        q_ref, k_ref, v_ref, mixed_ref, exact_ref, totals_ref = refs; kp = qp = None
    keys, group = k_ref.shape; queries = q_ref.shape[0]; tile = key_tile(keys)
    heads = group // HEAD_DIM
    q = (q_ref[...].astype(F32) * SCALING).astype(BF16)
    starts = range(0, keys, tile)
    qs = [only_head(q, h, group) for h in range(heads)]
    scores = [[None] * len(starts) for _ in range(heads)]
    tops = [None] * heads
    for i, start in enumerate(starts):
        ok = visible(tile, queries, start, used, half, kp, qp)
        for h in range(heads):
            s = mm(k_ref[start:start+tile, :], qs[h], 1, 1)
            if ok is not None: s = jnp.where(ok, s, -1e30)
            m = jnp.max(s, axis=0, keepdims=True)
            tops[h] = m if tops[h] is None else jnp.maximum(tops[h], m)
            scores[h][i] = s
    totals = [None] * heads; accs = [None] * heads
    for i, start in enumerate(starts):
        for h in range(heads):
            e = jnp.exp(scores[h][i] - tops[h])
            es = jnp.sum(e, axis=0, keepdims=True)
            o = mm(v_ref[start:start+tile, :], e.astype(BF16), 0, 0)
            totals[h] = es if totals[h] is None else totals[h] + es
            accs[h] = o if accs[h] is None else accs[h] + o
    for h in range(heads):
        rows = slice(h*HEAD_DIM, (h+1)*HEAD_DIM)
        exact_ref[rows, :] = accs[h][rows, :] * (1.0/totals[h])
        totals_ref[0, h:h+1, :] = tops[h] + jnp.log(totals[h])
    mixed_ref[...] = exact_ref[...].T.astype(BF16)

def backward_kernel(used, half, causal, kept, *refs):
    refs = refs[: len(refs) - 3 - kept] + refs[len(refs) - 3 :]
    if causal:
        kp, qp, q_ref, k_ref, v_ref, g_ref, exact_ref, totals_ref, dq_ref, dk_ref, dv_ref = refs
    else:
        q_ref, k_ref, v_ref, g_ref, exact_ref, totals_ref, dq_ref, dk_ref, dv_ref = refs; kp = qp = None
    keys, group = k_ref.shape; queries = q_ref.shape[0]; tile = key_tile(keys)
    heads = group // HEAD_DIM
    q = (q_ref[...].astype(F32) * SCALING).astype(BF16)
    g = g_ref[...]
    both = exact_ref[...] * g.astype(F32).T
    qs = [only_head(q, h, group) for h in range(heads)]
    gs = [only_head(g, h, group) for h in range(heads)]
    dots = [jnp.sum(both[h*HEAD_DIM:(h+1)*HEAD_DIM, :], axis=0, keepdims=True) for h in range(heads)]
    dqs = [None]*heads
    for start in range(0, keys, tile):
        k = k_ref[start:start+tile, :]; v = v_ref[start:start+tile, :]
        ok = visible(tile, queries, start, used, half, kp, qp)
        dk = dv = None
        for h in range(heads):
            s = mm(k, qs[h], 1, 1)
            if ok is not None: s = jnp.where(ok, s, -1e30)
            p = jnp.exp(s - totals_ref[0, h:h+1, :])
            dp = mm(v, gs[h], 1, 1)
            ds = (p * (dp - dots[h])).astype(BF16)
            a = mm(ds, qs[h], 1, 0); b = mm(p.astype(BF16), gs[h], 1, 0)
            dk = a if dk is None else dk + a
            dv = b if dv is None else dv + b
            c = mm(k, ds, 0, 0)
            dqs[h] = c if dqs[h] is None else dqs[h] + c
        dk_ref[start:start+tile, :] = dk.astype(BF16)
        dv_ref[start:start+tile, :] = dv.astype(BF16)
    full = jnp.concatenate([dqs[h][h*HEAD_DIM:(h+1)*HEAD_DIM, :] for h in range(heads)], axis=0)
    dq_ref[...] = (full.T * SCALING).astype(BF16)

def attend_forward(q, k, v, used, half, places=None):
    queries, width = q.shape; keys = k.shape[0]; group = min(128, width); n = width//group
    col = lambda rows: pl.BlockSpec((rows, group), lambda i: (0, i))
    fixed = lambda shape: pl.BlockSpec(shape, lambda i: (0, 0))
    extra = [] if places is None else list(places)
    return pl.pallas_call(
        functools.partial(forward_kernel, used, half, places is not None),
        grid=(n,),
        in_specs=[fixed(p.shape) for p in extra]+[col(queries), col(keys), col(keys)],
        out_specs=[col(queries), pl.BlockSpec((group, queries), lambda i: (i, 0)), pl.BlockSpec((1, group//HEAD_DIM, queries), lambda i: (i,0,0))],
        out_shape=[jax.ShapeDtypeStruct((queries,width),BF16), jax.ShapeDtypeStruct((width,queries),F32), jax.ShapeDtypeStruct((n,group//HEAD_DIM,queries),F32)],
        compiler_params=pltpu.CompilerParams(vmem_limit_bytes=20 * 2**20),
    )(*extra, q, k, v)

def attend_backward(q, k, v, g, exact, totals, used, half, places=None, only=None, into=()):
    queries, width = q.shape
    keys, group = k.shape[0], min(128, width)
    count = width // group
    first = 0 if only is None else only

    def columns(rows):
        return pl.BlockSpec((rows, group), lambda i: (0, first + i))

    def fixed(shape):
        return pl.BlockSpec(shape, lambda i: (0, 0))

    extra = [] if places is None else list(places)
    operands = [*extra, q, k, v, g, exact, totals]
    shapes = [(queries, width), (keys, width), (keys, width)]
    return pl.pallas_call(
        functools.partial(backward_kernel, used, half, places is not None, len(into)),
        grid=(count if only is None else 1,),
        in_specs=[fixed(place.shape) for place in extra]
        + [columns(queries), columns(keys), columns(keys), columns(queries)]
        + [pl.BlockSpec((group, queries), lambda i: (first + i, 0))]
        + [pl.BlockSpec((1, group // HEAD_DIM, queries), lambda i: (first + i, 0, 0))]
        + [pl.BlockSpec(memory_space=pl.ANY)] * len(into),
        out_specs=[columns(rows) for rows, _ in shapes],
        out_shape=[jax.ShapeDtypeStruct(shape, BF16) for shape in shapes],
        input_output_aliases={len(operands) + i: i for i in range(len(into))},
        compiler_params=pltpu.CompilerParams(vmem_limit_bytes=20 * 2**20),
    )(*operands, *into)


def weight_grads_kernel(count, order_ref, which_ref, *refs):
    out_ref, start = refs[-1], 0
    rows = out_ref.shape[2]
    step = pl.program_id(0)
    for i in range(count):
        left, right = refs[i], refs[count + i]
        stop = start + right.shape[1]
        total = mm(left[...], right[...], 0, 0).astype(BF16)
        devices = total.shape[0] // (2 * rows)
        for j in range(devices):
            place = order_ref[step * devices + j]
            for half in range(2):
                row = (2 * j + half) * rows
                out_ref[place, (which_ref[0] == half).astype(jnp.int32), :, start:stop] = total[
                    row : row + rows, :
                ]
        start = stop


def weight_grads(order, which, pairs, columns=1, into=None):
    steps, width = order.shape[0], pairs[0][0].shape[1]
    rows, total = width // steps, sum(right.shape[1] for _, right in pairs)
    count, tile = len(pairs), max(256, rows)
    out = (steps, 2, rows // 2, total * columns)
    column = columns - 1 if into is None else 0
    kept = () if into is None else (into,)
    return pl.pallas_call(
        functools.partial(weight_grads_kernel, count),
        grid_spec=pltpu.PrefetchScalarGridSpec(
            num_scalar_prefetch=2,
            grid=(width // tile,),
            in_specs=[
                pl.BlockSpec((left.shape[0], tile), lambda i, order, which: (0, i))
                for left, _ in pairs
            ]
            + [pl.BlockSpec(right.shape, lambda i, order, which: (0, 0)) for _, right in pairs]
            + [pl.BlockSpec(memory_space=pl.ANY)] * len(kept),
            out_specs=pl.BlockSpec(
                out[:3] + (total,), lambda i, order, which: (0, 0, 0, column)
            ),
        ),
        out_shape=jax.ShapeDtypeStruct(out, BF16),
        input_output_aliases={2 + 2 * count: 0} if kept else {},
        compiler_params=pltpu.CompilerParams(vmem_limit_bytes=20 * 2**20),
    )(order, which, *[left for left, _ in pairs], *[right for _, right in pairs], *kept)


def ring_add_kernel(counts, *refs):
    ins, outs = refs[: len(refs) - len(counts)], refs[len(refs) - len(counts) :]
    at = 0
    for count, out_ref in zip(counts, outs):
        moved, start = ins[at], 0
        for part in ins[at + 1 : at + 1 + count]:
            stop = start + part.shape[1]
            total = moved[:, start:stop].astype(F32) + part[...].astype(F32)
            out_ref[:, start:stop] = total.astype(BF16)
            start = stop
        at += 1 + count


def ring_add(items):
    specs, operands = [], []
    for moved, parts, distance, half in items:
        specs.append(pl.BlockSpec(memory_space=pltpu.VMEM))
        operands.append(moved)
        for part in parts:
            block = (None, None) + part.shape[2:]
            specs.append(pl.BlockSpec(block, lambda i, d=distance, h=half: (d, h, 0, 0)))
            operands.append(part)
    return pl.pallas_call(
        functools.partial(ring_add_kernel, [len(parts) for _, parts, _, _ in items]),
        grid=(1,),
        in_specs=specs,
        out_specs=[pl.BlockSpec(memory_space=pltpu.VMEM)] * len(items),
        out_shape=[jax.ShapeDtypeStruct(moved.shape, BF16) for moved, _, _, _ in items],
        compiler_params=pltpu.CompilerParams(vmem_limit_bytes=6 * 2**20),
    )(*operands)


def pack_kernel(count, which_ref, *refs):
    mine_ref, other_ref = refs[count:]
    for mine in range(2):

        @pl.when(which_ref[0] == mine)
        def _():
            start = 0
            for ref in refs[:count]:
                size = ref.shape[2] // 2
                for k in range(ref.shape[0]):
                    piece = ref[k]
                    for out_ref, index in ((mine_ref, mine), (other_ref, 1 - mine)):
                        out_ref[:, start : start + size] = piece[:, index * size : (index + 1) * size]
                    start += size


def pack(which, weights):
    rows = weights[0].shape[1]
    total = sum(weight.shape[0] * (weight.shape[2] // 2) for weight in weights)
    shape = jax.ShapeDtypeStruct((rows, total), BF16)
    return pl.pallas_call(
        functools.partial(pack_kernel, len(weights)),
        in_specs=[pl.BlockSpec(memory_space=pltpu.SMEM)]
        + [pl.BlockSpec(memory_space=pltpu.VMEM)] * len(weights),
        out_specs=[pl.BlockSpec(memory_space=pltpu.VMEM)] * 2,
        out_shape=[shape, shape],
        compiler_params=pltpu.CompilerParams(vmem_limit_bytes=6 * 2**20),
    )(which, *weights)


def unpack_kernel(counts, which_ref, mine_ref, theirs_ref, *out_refs):
    for mine in range(2):

        @pl.when(which_ref[0] == mine)
        def _():
            start = 0
            for ref, count in zip(out_refs, counts):
                size = ref.shape[2] // 2
                for k in range(count):
                    for in_ref, index in ((mine_ref, mine), (theirs_ref, 1 - mine)):
                        ref[k, :, index * size : (index + 1) * size] = in_ref[
                            :, start : start + size
                        ].astype(F32)
                    start += size


def unpack(which, mine, theirs, spans):
    rows = mine.shape[0]
    return pl.pallas_call(
        functools.partial(unpack_kernel, [count for count, _ in spans]),
        in_specs=[pl.BlockSpec(memory_space=pltpu.SMEM)]
        + [pl.BlockSpec(memory_space=pltpu.VMEM)] * 2,
        out_specs=[pl.BlockSpec(memory_space=pltpu.VMEM)] * len(spans),
        out_shape=[jax.ShapeDtypeStruct((count, rows, 2 * size), F32) for count, size in spans],
        compiler_params=pltpu.CompilerParams(vmem_limit_bytes=6 * 2**20),
    )(which, mine, theirs)


def assemble_kernel(count, spans, places_ref, *refs):
    pieces, outs, sems = refs[:count], refs[count:-1], refs[-1]
    rows = pieces[0].shape[0]

    def copies():
        for i in range(count):
            row = pl.multiple_of(places_ref[i] * rows, rows)
            start = 0
            for k, (size, out_ref) in enumerate(zip(spans, outs)):
                yield pltpu.make_async_copy(
                    pieces[i].at[:, start : start + size],
                    out_ref.at[pl.ds(row, rows), :],
                    sems.at[i * len(spans) + k],
                )
                start += size

    for copy in copies():
        copy.start()
    for copy in copies():
        copy.wait()


def assemble(places, pieces, spans):
    rows, count = pieces[0].shape[0], len(pieces)
    return pl.pallas_call(
        functools.partial(assemble_kernel, count, spans),
        in_specs=[pl.BlockSpec(memory_space=pltpu.SMEM)]
        + [pl.BlockSpec(memory_space=pl.ANY)] * count,
        out_specs=[pl.BlockSpec(memory_space=pltpu.VMEM)] * len(spans),
        out_shape=[jax.ShapeDtypeStruct((rows * count, size), BF16) for size in spans],
        scratch_shapes=[pltpu.SemaphoreType.DMA((count * len(spans),))],
        compiler_params=pltpu.CompilerParams(vmem_limit_bytes=16 * 2**20),
    )(places, *pieces)


def layer_norm(values, scales, shifts):
    row_mean = jnp.mean(values, axis=-1, keepdims=True)
    centred = values - row_mean
    variance = jnp.mean(centred * centred, axis=-1, keepdims=True)
    inverse = lax.rsqrt(variance + 1e-05)
    hat = centred * inverse
    return hat * scales + shifts, hat, inverse


def norm_back(hat, inverse, scales, incoming):
    scaled = incoming * scales
    return (
        scaled
        - jnp.mean(scaled, axis=-1, keepdims=True)
        - hat * jnp.mean(scaled * hat, axis=-1, keepdims=True)
    ) * inverse


def advance(rider, value):
    try:
        return [(rider,) + rider.send(value)]
    except StopIteration:
        return []


def build(fsdp, ctx, tp):
    assert ctx == 2
    ring = list(range(0, fsdp, 2)) + list(range(fsdp - 1, 0, -2)) if fsdp > 1 else [0]
    onward = [(ring[i], ring[(i + 1) % fsdp]) for i in range(fsdp)]
    backward_ring = [(b, a) for a, b in onward]
    swap = [(0, 1), (1, 0)]
    on_across = [(2 * a + c, 2 * b + 1 - c) for a, b in onward for c in range(2)]
    back_across = [(2 * a + c, 2 * b + 1 - c) for a, b in backward_ring for c in range(2)]

    def ring_place(index):
        return jnp.where(index % 2 == 0, index // 2, fsdp - 1 - index // 2)

    def ring_index(place):
        place = place % fsdp
        return jnp.where(2 * place < fsdp, 2 * place, 2 * fsdp - 1 - 2 * place)

    def ctx_swap(values):
        return lax.ppermute(values, "ctx", swap)

    def tp_swap(values):
        return lax.ppermute(values, "tp", swap)

    def ordered(first, second, index, axis):
        return jnp.where(
            index == 0,
            jnp.concatenate((first, second), axis=axis),
            jnp.concatenate((second, first), axis=axis),
        )

    def after(values, token):
        return lax.optimization_barrier((values, token))[0]

    def per_device(
        inputs,
        encoder_states,
        self_weights,
        self_output,
        cross_query,
        cross_memory,
        cross_output,
        hidden_in,
        hidden_out,
        norm_gains,
        norm_shifts,
        head_biases,
        output_biases,
        hidden_bias,
        cotangent,
    ):
        f, c, t = lax.axis_index("fsdp"), lax.axis_index("ctx"), lax.axis_index("tp")
        place = ring_place(f)
        rows, width = inputs.shape[1], inputs.shape[2]
        part = rows // tp
        half_rows = ctx * part
        shard = self_weights.shape[0]
        q_self = self_weights.shape[2] // ctx
        q_hidden = hidden_in.shape[1] // ctx

        def all_halves(half):
            if tp == 2:
                return jnp.concatenate((half, tp_swap(half)), axis=0)
            return lax.all_gather(half, "tp", axis=0, tiled=True)

        def own_half(values):
            if tp == 2:
                return values[:half_rows]
            return lax.dynamic_slice_in_dim(values, t * half_rows, half_rows, axis=0)

        def own_part(half):
            return lax.dynamic_slice_in_dim(half, c * part, part, axis=0)

        def group_sum(partial, hook=lambda mine: mine):
            if tp == 2:
                mine = partial[:half_rows] + tp_swap(partial[half_rows:].astype(BF16)).astype(F32)
            else:
                mine = lax.psum_scatter(
                    partial.astype(BF16), "tp", scatter_dimension=0, tiled=True
                )
            mine = hook(mine.astype(BF16))
            return mine.astype(F32) + ctx_swap(mine).astype(F32)

        def chip_rows(half):
            own = own_part(half)
            if tp == 2:
                return ordered(own, tp_swap(own), t, 0)
            return lax.all_gather(own, "tp", axis=0, tiled=True)

        def half_of(values):
            own = lax.dynamic_slice_in_dim(values, t * part, part, axis=0)
            return ordered(own, ctx_swap(own), c, 0)

        which = c.astype(jnp.int32).reshape(1)
        steps = jnp.arange(fsdp, dtype=jnp.int32)
        piece_places = jnp.stack(
            (
                ring_index(place + fsdp - steps) * ctx + c,
                ring_index(place + steps) * ctx + 1 - c,
            ),
            axis=1,
        ).reshape(-1)
        piece_places = piece_places.astype(jnp.int32)

        ring_order = ((ring_place(steps) - place) % fsdp).astype(jnp.int32)

        class GatherRing:
            def __init__(self, mine, other):
                self.first = (mine, other)
                self.trail = [(mine, ctx_swap(other))]

            def turn(self, values=()):
                if len(self.trail) == 1:
                    mine, other = self.first
                    other = lax.ppermute(other, ("fsdp", "ctx"), back_across)
                else:
                    mine, other = self.trail[-1]
                    other = lax.ppermute(other, "fsdp", backward_ring)
                mine = lax.ppermute(mine, "fsdp", onward)
                mine, other, values = lax.optimization_barrier((mine, other, values))
                self.trail.append((mine, other))
                return values

            def finish(self, spans):
                while len(self.trail) < fsdp:
                    self.turn()
                pieces = [piece for pair in self.trail for piece in pair]
                if all(size % 128 == 0 for size in spans):
                    return assemble(piece_places, pieces, spans)
                (full,) = assemble(piece_places, pieces, [sum(spans)])
                stops = [sum(spans[: i + 1]) for i in range(len(spans))]
                return [full[:, stop - size : stop] for size, stop in zip(spans, stops)]

        class ScatterRing:
            def __init__(self, blocks):
                self.blocks = blocks
                self.theirs, self.mine = blocks[fsdp - 1, 0], blocks[1 % fsdp, 1]
                self.step = 1

            def send(self):
                moved = [lax.ppermute(self.mine, "fsdp", backward_ring)]
                if self.step < fsdp - 1:
                    moved.append(lax.ppermute(self.theirs, "fsdp", onward))
                else:
                    moved.append(lax.ppermute(self.theirs, ("fsdp", "ctx"), on_across))
                if self.step == fsdp - 2:
                    moved.append(ctx_swap(self.blocks[0, 0]))
                return moved

            def add(self, moved):
                if self.step == fsdp - 2:
                    self.swapped = moved[2]
                more = self.blocks[(1 + self.step) % fsdp, 1]
                self.mine = (moved[0].astype(F32) + more.astype(F32)).astype(BF16)
                more = self.swapped if self.step == fsdp - 1 else self.blocks[fsdp - 1 - self.step, 0]
                self.theirs = (moved[1].astype(F32) + more.astype(F32)).astype(BF16)
                self.step += 1

        waiting = []

        def launch(rider):
            waiting.extend(advance(rider, None))

        def turn(rings, values=()):
            rings = [ring for ring in rings if ring.step < fsdp]
            due = [item for item in waiting if item[2] <= 1]
            waiting[:] = [(rider, v, left - 1) for rider, v, left in waiting if left > 1]
            moved, arrived, values = lax.optimization_barrier(
                ([ring.send() for ring in rings], [value for _, value, _ in due], values)
            )
            for ring, pair in zip(rings, moved):
                ring.add(pair)
            for item, value in zip(due, arrived):
                waiting.extend(advance(item[0], value))
            return values

        def finish(rings):
            while waiting or any(ring.step < fsdp for ring in rings):
                turn(rings)

        mine, other = pack(
            which,
            [
                jnp.transpose(self_weights, (1, 0, 2)),
                jnp.transpose(cross_memory, (1, 0, 2)),
                self_output.T[None],
                cross_query[None],
                cross_output.T[None],
            ],
        )
        ring = GatherRing(mine, other)
        trail = ring.trail
        w_qkv, w_memory, w_self_out, w_query, w_cross_out = ring.finish(
            [3 * q_self, 2 * q_self, q_self, q_self, q_self]
        )
        token_half = half_of(after(inputs[0], trail[1]))
        frames_here = after(encoder_states[0], trail[2])
        mine, other = pack(which, [hidden_in[None], hidden_out.T[None]])
        hidden_ring = GatherRing(*after((mine, other), trail[fsdp - 2]))
        cot_here = after(cotangent[0], trail[-2])
        def my_bias(bias):
            return lax.dynamic_index_in_dim(
                bias.reshape(bias.shape[:-1] + (ctx, -1)), c, bias.ndim - 1, keepdims=False
            )

        head_bias = my_bias(head_biases)
        hidden_own_bias = my_bias(hidden_bias)

        tokens = all_halves(token_half).astype(F32)
        frame_rows = frames_here.shape[0]
        frame_half = -(-frame_rows // 256) * 256
        piece = ctx_swap(
            lax.dynamic_slice_in_dim(frames_here, t * (width // tp), width // tp, axis=1)
        )
        if tp == 2:
            frames_there = ordered(piece, tp_swap(piece), t, 1)
        else:
            frames_there = lax.all_gather(piece, "tp", axis=1, tiled=True)
        blank = ((0, frame_half - frame_rows), (0, 0))
        frames = jnp.concatenate((jnp.pad(frames_here, blank), jnp.pad(frames_there, blank)), axis=0)
        cot_half = half_of(cot_here)
        cot_all = all_halves(cot_half)
        stream_half = own_half(tokens)

        normed_one, hat_one, inverse_one = layer_norm(tokens, norm_gains[0], norm_shifts[0])
        normed_one = normed_one.astype(BF16)
        projected = mm(normed_one, w_qkv, 1, 0)
        (projected,) = hidden_ring.turn((projected,))
        queries = (projected[:, :q_self] + head_bias[0]).astype(BF16)
        self_keys = projected[:, q_self : 2 * q_self].astype(BF16)
        self_values = (projected[:, 2 * q_self :] + head_bias[1]).astype(BF16)
        j = jnp.arange(ctx * rows, dtype=jnp.int32)
        jt, jc, i = j // half_rows, (j // part) % ctx, j % part
        if tp == 2:
            jt = jt ^ t
        position = jc * rows + jt * part + i
        places = (position[:, None], position[None, :])
        self_mixed, self_exact, self_totals = attend_forward(
            queries, self_keys, self_values, ctx * rows, ctx * rows, places
        )
        memory_bias = jnp.concatenate((jnp.zeros((q_self,), F32), head_bias[3]))
        frame_proj = (mm(frames, w_memory, 1, 0) + memory_bias).astype(BF16)
        (frame_proj,) = hidden_ring.turn((frame_proj,))
        after_self = stream_half + (
            group_sum(mm(self_mixed, w_self_out, 1, 1))
            + output_biases[0]
        )
        (after_self,) = hidden_ring.turn((after_self,))
        normed_two, hat_two, inverse_two = layer_norm(after_self, norm_gains[1], norm_shifts[1])
        normed_two = all_halves(normed_two.astype(BF16))
        cross_queries = (mm(normed_two, w_query, 1, 0) + head_bias[2]).astype(BF16)
        (cross_queries,) = hidden_ring.turn((cross_queries,))
        frame_keys, frame_values = frame_proj[:, :q_self], frame_proj[:, q_self:]
        cross_mixed, cross_exact, cross_totals = attend_forward(
            cross_queries, frame_keys, frame_values, frame_rows, frame_half
        )
        after_cross = after_self + (
            group_sum(mm(cross_mixed, w_cross_out, 1, 1)) + output_biases[1]
        )
        normed_three, hat_three, inverse_three = layer_norm(
            after_cross, norm_gains[2], norm_shifts[2]
        )
        normed_three = all_halves(normed_three.astype(BF16))
        w_in, w_out = hidden_ring.finish([q_hidden, q_hidden])
        pre_gelu = mm(normed_three, w_in, 1, 0) + hidden_own_bias
        cdf = 0.5 * (1.0 + lax.erf(pre_gelu * (0.5**0.5)))
        activated = (pre_gelu * cdf).astype(BF16)
        slope = cdf + pre_gelu * jnp.exp(-0.5 * pre_gelu * pre_gelu) * 0.3989422804014327

        grad_pre = (mm(cot_all, w_out, 1, 0) * slope).astype(BF16)
        grad_three = group_sum(mm(grad_pre, w_in, 1, 1))
        hidden_total = group_sum(mm(activated, w_out, 1, 1))
        output_half = (after_cross + (hidden_total + output_biases[2])).astype(BF16)
        layer_output = chip_rows(output_half)[None]
        done = {}
        grad_hidden = weight_grads(ring_order, which, [(normed_three, grad_pre), (cot_all, activated)])
        hidden_ring = ScatterRing(grad_hidden)
        grad_three = after(grad_three, grad_hidden)
        grad_after_cross = cot_half.astype(F32) + norm_back(
            hat_three, inverse_three, norm_gains[2], grad_three
        )
        grad_cross_half = grad_after_cross.astype(BF16)
        grad_cross = all_halves(grad_cross_half)

        grad_cross_mixed = mm(grad_cross, w_cross_out, 1, 0).astype(BF16)
        cross_grads = ()
        for only in range(max(1, q_self // 128)):
            cross_grads = attend_backward(
                cross_queries,
                frame_keys,
                frame_values,
                grad_cross_mixed,
                cross_exact,
                cross_totals,
                frame_rows,
                frame_half,
                only=only,
                into=tuple(cross_grads),
            )
            cross_grads = turn([hidden_ring], tuple(cross_grads))
        grad_cross_queries, grad_fkeys, grad_fvalues = cross_grads
        grad_two = group_sum(mm(grad_cross_queries, w_query, 1, 1))
        grad_frames = jnp.concatenate((grad_fkeys, grad_fvalues), axis=1)
        cross_blocks = weight_grads(
            ring_order,
            which,
            [(frames, grad_frames), (grad_cross, cross_mixed), (normed_two, grad_cross_queries)],
            columns=2,
        )
        (grad_two,) = turn([hidden_ring], (after(grad_two, cross_blocks),))
        grad_after_self = grad_after_cross + norm_back(
            hat_two, inverse_two, norm_gains[1], grad_two
        )
        grad_self_half = grad_after_self.astype(BF16)
        grad_self = all_halves(grad_self_half)

        grad_self_mixed = mm(grad_self, w_self_out, 1, 0).astype(BF16)
        grad_queries, grad_keys, grad_values = attend_backward(
            queries,
            self_keys,
            self_values,
            grad_self_mixed,
            self_exact,
            self_totals,
            ctx * rows,
            ctx * rows,
            places,
        )
        (grad_queries,) = turn([hidden_ring], (grad_queries,))
        grad_projected = jnp.concatenate((grad_queries, grad_keys, grad_values), axis=1)
        self_blocks = weight_grads(
            ring_order,
            which,
            [(normed_one, grad_projected), (grad_self, self_mixed)],
            columns=2,
            into=cross_blocks,
        )

        def column_sum(values):
            return jnp.sum(values.astype(F32), axis=0)

        def tokens_rider():
            partial = mm(grad_projected, w_qkv, 1, 1)
            if tp == 2:
                moved = yield tp_swap(partial[half_rows:].astype(BF16)), 1
                mine = (partial[:half_rows] + moved.astype(F32)).astype(BF16)
            else:
                mine = lax.psum_scatter(
                    partial.astype(BF16), "tp", scatter_dimension=0, tiled=True
                )
            moved = yield ctx_swap(mine), 2
            grad_one = mine.astype(F32) + moved.astype(F32)
            hat, inverse = own_half(hat_one), own_half(inverse_one)
            total = own_part(grad_after_self + norm_back(hat, inverse, norm_gains[0], grad_one))
            wide = jnp.stack(
                (
                    column_sum(grad_one * hat),
                    column_sum(hat_two * grad_two),
                    column_sum(hat_three * grad_three),
                    column_sum(grad_one),
                    column_sum(grad_two),
                    column_sum(grad_three),
                    column_sum(grad_self_half),
                    column_sum(grad_cross_half),
                    column_sum(cot_half),
                )
            )
            if tp == 2:
                moved, other_rows = yield (tp_swap(wide), tp_swap(total)), 1
                wide = wide + moved
                done["inputs"] = ordered(total, other_rows, t, 0)[None]
            else:
                wide = lax.psum(wide, "tp")
                done["inputs"] = lax.all_gather(total, "tp", axis=0, tiled=True)[None]
            narrow = jnp.concatenate(
                (
                    column_sum(grad_queries),
                    column_sum(grad_values),
                    column_sum(grad_cross_queries),
                    column_sum(grad_fvalues),
                    column_sum(grad_pre),
                )
            )
            small = jnp.concatenate((wide.reshape(-1), narrow))
            hop = 1
            while hop < fsdp:
                moved = yield lax.ppermute(small, "fsdp", [(i, i ^ hop) for i in range(fsdp)]), 1
                small = small + moved
                hop *= 2
            done["wide"] = small[: 9 * width].reshape(9, width)
            narrow = small[9 * width :]
            moved = yield ctx_swap(narrow), 1
            done["narrow"] = ordered(narrow[None], moved[None], c, 0)

        ring = ScatterRing(self_blocks)
        def frames_rider():
            encoder_part = mm(grad_frames, w_memory, 1, 1).astype(BF16)
            if tp == 2:
                half = width // 2
                keep = lax.dynamic_slice_in_dim(encoder_part, t * half, half, axis=1)
                give = lax.dynamic_slice_in_dim(encoder_part, (1 - t) * half, half, axis=1)
                moved = yield tp_swap(give), 1
                total = (keep.astype(F32) + moved.astype(F32)).astype(BF16)
            else:
                total = lax.psum_scatter(encoder_part, "tp", scatter_dimension=1, tiled=True)
            moved = yield ctx_swap(total[frame_half : frame_half + frame_rows]), 3
            done["frames"] = (total[:frame_rows].astype(F32) + moved.astype(F32))[None]

        launch(tokens_rider())
        launch(frames_rider())
        finish([hidden_ring, ring])
        grad_hidden_in, grad_hidden_out = unpack(
            which,
            hidden_ring.mine,
            hidden_ring.theirs,
            [(1, q_hidden), (1, q_hidden)],
        )
        (
            grad_self_weights,
            grad_self_output,
            grad_memory,
            grad_cross_output,
            grad_cross_query,
        ) = unpack(
            which,
            ring.mine,
            ring.theirs,
            [(3, q_self), (1, q_self), (2, q_self), (1, q_self), (1, q_self)],
        )
        grad_inputs, grad_encoder, wide = done["inputs"], done["frames"], done["wide"]
        both = done["narrow"]
        grad_head = both[:, : 4 * q_self].reshape(ctx, 4, q_self)
        grad_head = jnp.transpose(grad_head, (1, 0, 2)).reshape(4, -1)
        grad_hidden_bias = both[:, 4 * q_self :].reshape(-1)
        return (
            layer_output,
            grad_inputs,
            grad_encoder,
            jnp.transpose(grad_self_weights, (1, 0, 2)),
            grad_self_output[0].T,
            grad_cross_query[0],
            jnp.transpose(grad_memory, (1, 0, 2)),
            grad_cross_output[0].T,
            grad_hidden_in[0],
            grad_hidden_out[0].T,
            wide[0:3],
            wide[3:6],
            grad_head,
            wide[6:9],
            grad_hidden_bias,
        )

    return per_device


def solution(mesh):
    in_specs = (
        P("fsdp", "ctx", None),
        P("fsdp", "ctx", None),
        P(("fsdp", "ctx"), None, "tp"),
        P("tp", ("fsdp", "ctx")),
        P(("fsdp", "ctx"), "tp"),
        P(("fsdp", "ctx"), None, "tp"),
        P("tp", ("fsdp", "ctx")),
        P(("fsdp", "ctx"), "tp"),
        P("tp", ("fsdp", "ctx")),
        P(),
        P(),
        P(None, "tp"),
        P(),
        P("tp"),
        P("fsdp", "ctx", None),
    )
    out_specs = (
        P("fsdp", "ctx", None),
        P("fsdp", "ctx", None),
        P("fsdp", "ctx", "tp"),
        P(("fsdp", "ctx"), None, "tp"),
        P("tp", ("fsdp", "ctx")),
        P(("fsdp", "ctx"), "tp"),
        P(("fsdp", "ctx"), None, "tp"),
        P("tp", ("fsdp", "ctx")),
        P(("fsdp", "ctx"), "tp"),
        P("tp", ("fsdp", "ctx")),
        P(),
        P(),
        P(None, "tp"),
        P(),
        P("tp"),
    )
    per_device = build(mesh.shape["fsdp"], mesh.shape["ctx"], mesh.shape["tp"])
    return jax.shard_map(
        per_device, mesh=mesh, in_specs=in_specs, out_specs=out_specs, check_vma=False
    )
```

```python
import functools

import jax
import jax.numpy as jnp
from jax import lax
from jax.experimental import pallas as pl
from jax.experimental.pallas import tpu as pltpu
from jax.sharding import PartitionSpec as P

HEAD_DIM = 64
SCALING = HEAD_DIM ** (-0.5)
F32 = jnp.float32
BF16 = jnp.bfloat16


def key_tile(total):
    return 256 if total % 256 == 0 else total

def mm(left, right, left_dim, right_dim):
    return lax.dot_general(
        left, right, (((left_dim,), (right_dim,)), ((), ())), preferred_element_type=F32
    )

def only_head(values, head, group):
    if group == HEAD_DIM: return values
    lane = lax.broadcasted_iota(jnp.int32, values.shape, 1)
    return jnp.where(lane // HEAD_DIM == head, values, jnp.zeros_like(values))

def visible(tile, queries, start, used, half, key_place, query_place):
    if key_place is not None:
        return key_place[start:start+tile, :] <= query_place[...]
    row = start % half
    if row + tile > used:
        return row + lax.broadcasted_iota(jnp.int32, (tile, queries), 0) < used
    return None

def forward_kernel(used, half, causal, *refs):
    if causal:
        kp, qp, q_ref, k_ref, v_ref, mixed_ref, exact_ref, totals_ref = refs
    else:
        q_ref, k_ref, v_ref, mixed_ref, exact_ref, totals_ref = refs; kp = qp = None
    keys, group = k_ref.shape; queries = q_ref.shape[0]; tile = key_tile(keys)
    heads = group // HEAD_DIM
    q = (q_ref[...].astype(F32) * SCALING).astype(BF16)
    starts = range(0, keys, tile)
    qs = [only_head(q, h, group) for h in range(heads)]
    scores = [[None] * len(starts) for _ in range(heads)]
    tops = [None] * heads
    for i, start in enumerate(starts):
        ok = visible(tile, queries, start, used, half, kp, qp)
        for h in range(heads):
            s = mm(k_ref[start:start+tile, :], qs[h], 1, 1)
            if ok is not None: s = jnp.where(ok, s, -1e30)
            m = jnp.max(s, axis=0, keepdims=True)
            tops[h] = m if tops[h] is None else jnp.maximum(tops[h], m)
            scores[h][i] = s
    totals = [None] * heads; accs = [None] * heads
    for i, start in enumerate(starts):
        for h in range(heads):
            e = jnp.exp(scores[h][i] - tops[h])
            es = jnp.sum(e, axis=0, keepdims=True)
            o = mm(v_ref[start:start+tile, :], e.astype(BF16), 0, 0)
            totals[h] = es if totals[h] is None else totals[h] + es
            accs[h] = o if accs[h] is None else accs[h] + o
    for h in range(heads):
        rows = slice(h*HEAD_DIM, (h+1)*HEAD_DIM)
        exact_ref[rows, :] = accs[h][rows, :] * (1.0/totals[h])
        totals_ref[0, h:h+1, :] = tops[h] + jnp.log(totals[h])
    mixed_ref[...] = exact_ref[...].T.astype(BF16)

def backward_kernel(used, half, causal, kept, *refs):
    refs = refs[: len(refs) - 3 - kept] + refs[len(refs) - 3 :]
    if causal:
        kp, qp, q_ref, k_ref, v_ref, g_ref, exact_ref, totals_ref, dq_ref, dk_ref, dv_ref = refs
    else:
        q_ref, k_ref, v_ref, g_ref, exact_ref, totals_ref, dq_ref, dk_ref, dv_ref = refs; kp = qp = None
    keys, group = k_ref.shape; queries = q_ref.shape[0]; tile = key_tile(keys)
    heads = group // HEAD_DIM
    q = (q_ref[...].astype(F32) * SCALING).astype(BF16)
    g = g_ref[...]
    both = exact_ref[...] * g.astype(F32).T
    qs = [only_head(q, h, group) for h in range(heads)]
    gs = [only_head(g, h, group) for h in range(heads)]
    dots = [jnp.sum(both[h*HEAD_DIM:(h+1)*HEAD_DIM, :], axis=0, keepdims=True) for h in range(heads)]
    dqs = [None]*heads
    for start in range(0, keys, tile):
        k = k_ref[start:start+tile, :]; v = v_ref[start:start+tile, :]
        ok = visible(tile, queries, start, used, half, kp, qp)
        dk = dv = None
        for h in range(heads):
            s = mm(k, qs[h], 1, 1)
            if ok is not None: s = jnp.where(ok, s, -1e30)
            p = jnp.exp(s - totals_ref[0, h:h+1, :])
            dp = mm(v, gs[h], 1, 1)
            ds = (p * (dp - dots[h])).astype(BF16)
            a = mm(ds, qs[h], 1, 0); b = mm(p.astype(BF16), gs[h], 1, 0)
            dk = a if dk is None else dk + a
            dv = b if dv is None else dv + b
            c = mm(k, ds, 0, 0)
            dqs[h] = c if dqs[h] is None else dqs[h] + c
        dk_ref[start:start+tile, :] = dk.astype(BF16)
        dv_ref[start:start+tile, :] = dv.astype(BF16)
    full = jnp.concatenate([dqs[h][h*HEAD_DIM:(h+1)*HEAD_DIM, :] for h in range(heads)], axis=0)
    dq_ref[...] = (full.T * SCALING).astype(BF16)

def attend_forward(q, k, v, used, half, places=None):
    queries, width = q.shape; keys = k.shape[0]; group = min(128, width); n = width//group
    col = lambda rows: pl.BlockSpec((rows, group), lambda i: (0, i))
    fixed = lambda shape: pl.BlockSpec(shape, lambda i: (0, 0))
    extra = [] if places is None else list(places)
    return pl.pallas_call(
        functools.partial(forward_kernel, used, half, places is not None),
        grid=(n,),
        in_specs=[fixed(p.shape) for p in extra]+[col(queries), col(keys), col(keys)],
        out_specs=[col(queries), pl.BlockSpec((group, queries), lambda i: (i, 0)), pl.BlockSpec((1, group//HEAD_DIM, queries), lambda i: (i,0,0))],
        out_shape=[jax.ShapeDtypeStruct((queries,width),BF16), jax.ShapeDtypeStruct((width,queries),F32), jax.ShapeDtypeStruct((n,group//HEAD_DIM,queries),F32)],
        compiler_params=pltpu.CompilerParams(vmem_limit_bytes=20 * 2**20),
    )(*extra, q, k, v)

def attend_backward(q, k, v, g, exact, totals, used, half, places=None, only=None, into=()):
    queries, width = q.shape
    keys, group = k.shape[0], min(128, width)
    count = width // group
    first = 0 if only is None else only

    def columns(rows):
        return pl.BlockSpec((rows, group), lambda i: (0, first + i))

    def fixed(shape):
        return pl.BlockSpec(shape, lambda i: (0, 0))

    extra = [] if places is None else list(places)
    operands = [*extra, q, k, v, g, exact, totals]
    shapes = [(queries, width), (keys, width), (keys, width)]
    return pl.pallas_call(
        functools.partial(backward_kernel, used, half, places is not None, len(into)),
        grid=(count if only is None else 1,),
        in_specs=[fixed(place.shape) for place in extra]
        + [columns(queries), columns(keys), columns(keys), columns(queries)]
        + [pl.BlockSpec((group, queries), lambda i: (first + i, 0))]
        + [pl.BlockSpec((1, group // HEAD_DIM, queries), lambda i: (first + i, 0, 0))]
        + [pl.BlockSpec(memory_space=pl.ANY)] * len(into),
        out_specs=[columns(rows) for rows, _ in shapes],
        out_shape=[jax.ShapeDtypeStruct(shape, BF16) for shape in shapes],
        input_output_aliases={len(operands) + i: i for i in range(len(into))},
        compiler_params=pltpu.CompilerParams(vmem_limit_bytes=20 * 2**20),
    )(*operands, *into)


def weight_grads_kernel(count, order_ref, which_ref, *refs):
    out_ref, start = refs[-1], 0
    rows = out_ref.shape[2]
    step = pl.program_id(0)
    for i in range(count):
        left, right = refs[i], refs[count + i]
        stop = start + right.shape[1]
        total = mm(left[...], right[...], 0, 0).astype(BF16)
        devices = total.shape[0] // (2 * rows)
        for j in range(devices):
            place = order_ref[step * devices + j]
            for half in range(2):
                row = (2 * j + half) * rows
                out_ref[place, (which_ref[0] == half).astype(jnp.int32), :, start:stop] = total[
                    row : row + rows, :
                ]
        start = stop


def weight_grads(order, which, pairs, columns=1, into=None):
    steps, width = order.shape[0], pairs[0][0].shape[1]
    rows, total = width // steps, sum(right.shape[1] for _, right in pairs)
    count, tile = len(pairs), max(256, rows)
    out = (steps, 2, rows // 2, total * columns)
    column = columns - 1 if into is None else 0
    kept = () if into is None else (into,)
    return pl.pallas_call(
        functools.partial(weight_grads_kernel, count),
        grid_spec=pltpu.PrefetchScalarGridSpec(
            num_scalar_prefetch=2,
            grid=(width // tile,),
            in_specs=[
                pl.BlockSpec((left.shape[0], tile), lambda i, order, which: (0, i))
                for left, _ in pairs
            ]
            + [pl.BlockSpec(right.shape, lambda i, order, which: (0, 0)) for _, right in pairs]
            + [pl.BlockSpec(memory_space=pl.ANY)] * len(kept),
            out_specs=pl.BlockSpec(
                out[:3] + (total,), lambda i, order, which: (0, 0, 0, column)
            ),
        ),
        out_shape=jax.ShapeDtypeStruct(out, BF16),
        input_output_aliases={2 + 2 * count: 0} if kept else {},
        compiler_params=pltpu.CompilerParams(vmem_limit_bytes=20 * 2**20),
    )(order, which, *[left for left, _ in pairs], *[right for _, right in pairs], *kept)


def ring_add_kernel(counts, *refs):
    ins, outs = refs[: len(refs) - len(counts)], refs[len(refs) - len(counts) :]
    at = 0
    for count, out_ref in zip(counts, outs):
        moved, start = ins[at], 0
        for part in ins[at + 1 : at + 1 + count]:
            stop = start + part.shape[1]
            total = moved[:, start:stop].astype(F32) + part[...].astype(F32)
            out_ref[:, start:stop] = total.astype(BF16)
            start = stop
        at += 1 + count


def ring_add(items):
    specs, operands = [], []
    for moved, parts, distance, half in items:
        specs.append(pl.BlockSpec(memory_space=pltpu.VMEM))
        operands.append(moved)
        for part in parts:
            block = (None, None) + part.shape[2:]
            specs.append(pl.BlockSpec(block, lambda i, d=distance, h=half: (d, h, 0, 0)))
            operands.append(part)
    return pl.pallas_call(
        functools.partial(ring_add_kernel, [len(parts) for _, parts, _, _ in items]),
        grid=(1,),
        in_specs=specs,
        out_specs=[pl.BlockSpec(memory_space=pltpu.VMEM)] * len(items),
        out_shape=[jax.ShapeDtypeStruct(moved.shape, BF16) for moved, _, _, _ in items],
        compiler_params=pltpu.CompilerParams(vmem_limit_bytes=6 * 2**20),
    )(*operands)


def pack_kernel(count, which_ref, *refs):
    mine_ref, other_ref = refs[count:]
    for mine in range(2):

        @pl.when(which_ref[0] == mine)
        def _():
            start = 0
            for ref in refs[:count]:
                size = ref.shape[2] // 2
                for k in range(ref.shape[0]):
                    piece = ref[k]
                    for out_ref, index in ((mine_ref, mine), (other_ref, 1 - mine)):
                        out_ref[:, start : start + size] = piece[:, index * size : (index + 1) * size]
                    start += size


def pack(which, weights):
    rows = weights[0].shape[1]
    total = sum(weight.shape[0] * (weight.shape[2] // 2) for weight in weights)
    shape = jax.ShapeDtypeStruct((rows, total), BF16)
    return pl.pallas_call(
        functools.partial(pack_kernel, len(weights)),
        in_specs=[pl.BlockSpec(memory_space=pltpu.SMEM)]
        + [pl.BlockSpec(memory_space=pltpu.VMEM)] * len(weights),
        out_specs=[pl.BlockSpec(memory_space=pltpu.VMEM)] * 2,
        out_shape=[shape, shape],
        compiler_params=pltpu.CompilerParams(vmem_limit_bytes=6 * 2**20),
    )(which, *weights)


def unpack_kernel(counts, which_ref, mine_ref, theirs_ref, *out_refs):
    for mine in range(2):

        @pl.when(which_ref[0] == mine)
        def _():
            start = 0
            for ref, count in zip(out_refs, counts):
                size = ref.shape[2] // 2
                for k in range(count):
                    for in_ref, index in ((mine_ref, mine), (theirs_ref, 1 - mine)):
                        ref[k, :, index * size : (index + 1) * size] = in_ref[
                            :, start : start + size
                        ].astype(F32)
                    start += size


def unpack(which, mine, theirs, spans):
    rows = mine.shape[0]
    return pl.pallas_call(
        functools.partial(unpack_kernel, [count for count, _ in spans]),
        in_specs=[pl.BlockSpec(memory_space=pltpu.SMEM)]
        + [pl.BlockSpec(memory_space=pltpu.VMEM)] * 2,
        out_specs=[pl.BlockSpec(memory_space=pltpu.VMEM)] * len(spans),
        out_shape=[jax.ShapeDtypeStruct((count, rows, 2 * size), F32) for count, size in spans],
        compiler_params=pltpu.CompilerParams(vmem_limit_bytes=6 * 2**20),
    )(which, mine, theirs)


def assemble_kernel(count, spans, places_ref, *refs):
    pieces, outs, sems = refs[:count], refs[count:-1], refs[-1]
    rows = pieces[0].shape[0]

    def copies():
        for i in range(count):
            row = pl.multiple_of(places_ref[i] * rows, rows)
            start = 0
            for k, (size, out_ref) in enumerate(zip(spans, outs)):
                yield pltpu.make_async_copy(
                    pieces[i].at[:, start : start + size],
                    out_ref.at[pl.ds(row, rows), :],
                    sems.at[i * len(spans) + k],
                )
                start += size

    for copy in copies():
        copy.start()
    for copy in copies():
        copy.wait()


def assemble(places, pieces, spans):
    rows, count = pieces[0].shape[0], len(pieces)
    return pl.pallas_call(
        functools.partial(assemble_kernel, count, spans),
        in_specs=[pl.BlockSpec(memory_space=pltpu.SMEM)]
        + [pl.BlockSpec(memory_space=pl.ANY)] * count,
        out_specs=[pl.BlockSpec(memory_space=pltpu.VMEM)] * len(spans),
        out_shape=[jax.ShapeDtypeStruct((rows * count, size), BF16) for size in spans],
        scratch_shapes=[pltpu.SemaphoreType.DMA((count * len(spans),))],
        compiler_params=pltpu.CompilerParams(vmem_limit_bytes=16 * 2**20),
    )(places, *pieces)


def layer_norm(values, scales, shifts):
    row_mean = jnp.mean(values, axis=-1, keepdims=True)
    centred = values - row_mean
    variance = jnp.mean(centred * centred, axis=-1, keepdims=True)
    inverse = lax.rsqrt(variance + 1e-05)
    hat = centred * inverse
    return hat * scales + shifts, hat, inverse


def norm_back(hat, inverse, scales, incoming):
    scaled = incoming * scales
    return (
        scaled
        - jnp.mean(scaled, axis=-1, keepdims=True)
        - hat * jnp.mean(scaled * hat, axis=-1, keepdims=True)
    ) * inverse


def advance(rider, value):
    try:
        return [(rider,) + rider.send(value)]
    except StopIteration:
        return []


def build(fsdp, ctx, tp):
    assert ctx == 2
    ring = list(range(0, fsdp, 2)) + list(range(fsdp - 1, 0, -2)) if fsdp > 1 else [0]
    onward = [(ring[i], ring[(i + 1) % fsdp]) for i in range(fsdp)]
    backward_ring = [(b, a) for a, b in onward]
    swap = [(0, 1), (1, 0)]
    on_across = [(2 * a + c, 2 * b + 1 - c) for a, b in onward for c in range(2)]
    back_across = [(2 * a + c, 2 * b + 1 - c) for a, b in backward_ring for c in range(2)]

    def ring_place(index):
        return jnp.where(index % 2 == 0, index // 2, fsdp - 1 - index // 2)

    def ring_index(place):
        place = place % fsdp
        return jnp.where(2 * place < fsdp, 2 * place, 2 * fsdp - 1 - 2 * place)

    def ctx_swap(values):
        return lax.ppermute(values, "ctx", swap)

    def tp_swap(values):
        return lax.ppermute(values, "tp", swap)

    def ordered(first, second, index, axis):
        return jnp.where(
            index == 0,
            jnp.concatenate((first, second), axis=axis),
            jnp.concatenate((second, first), axis=axis),
        )

    def after(values, token):
        return lax.optimization_barrier((values, token))[0]

    def per_device(
        inputs,
        encoder_states,
        self_weights,
        self_output,
        cross_query,
        cross_memory,
        cross_output,
        hidden_in,
        hidden_out,
        norm_gains,
        norm_shifts,
        head_biases,
        output_biases,
        hidden_bias,
        cotangent,
    ):
        f, c, t = lax.axis_index("fsdp"), lax.axis_index("ctx"), lax.axis_index("tp")
        place = ring_place(f)
        rows, width = inputs.shape[1], inputs.shape[2]
        part = rows // tp
        half_rows = ctx * part
        shard = self_weights.shape[0]
        q_self = self_weights.shape[2] // ctx
        q_hidden = hidden_in.shape[1] // ctx

        def all_halves(half):
            if tp == 2:
                return jnp.concatenate((half, tp_swap(half)), axis=0)
            return lax.all_gather(half, "tp", axis=0, tiled=True)

        def own_half(values):
            if tp == 2:
                return values[:half_rows]
            return lax.dynamic_slice_in_dim(values, t * half_rows, half_rows, axis=0)

        def own_part(half):
            return lax.dynamic_slice_in_dim(half, c * part, part, axis=0)

        def group_sum(partial, hook=lambda mine: mine):
            if tp == 2:
                mine = partial[:half_rows] + tp_swap(partial[half_rows:].astype(BF16)).astype(F32)
            else:
                mine = lax.psum_scatter(
                    partial.astype(BF16), "tp", scatter_dimension=0, tiled=True
                )
            mine = hook(mine.astype(BF16))
            return mine.astype(F32) + ctx_swap(mine).astype(F32)

        def chip_rows(half):
            own = own_part(half)
            if tp == 2:
                return ordered(own, tp_swap(own), t, 0)
            return lax.all_gather(own, "tp", axis=0, tiled=True)

        def half_of(values):
            own = lax.dynamic_slice_in_dim(values, t * part, part, axis=0)
            return ordered(own, ctx_swap(own), c, 0)

        which = c.astype(jnp.int32).reshape(1)
        steps = jnp.arange(fsdp, dtype=jnp.int32)
        piece_places = jnp.stack(
            (
                ring_index(place + fsdp - steps) * ctx + c,
                ring_index(place + steps) * ctx + 1 - c,
            ),
            axis=1,
        ).reshape(-1)
        piece_places = piece_places.astype(jnp.int32)

        ring_order = ((ring_place(steps) - place) % fsdp).astype(jnp.int32)

        class GatherRing:
            def __init__(self, mine, other):
                self.first = (mine, other)
                self.trail = [(mine, ctx_swap(other))]

            def turn(self, values=()):
                if len(self.trail) == 1:
                    mine, other = self.first
                    other = lax.ppermute(other, ("fsdp", "ctx"), back_across)
                else:
                    mine, other = self.trail[-1]
                    other = lax.ppermute(other, "fsdp", backward_ring)
                mine = lax.ppermute(mine, "fsdp", onward)
                mine, other, values = lax.optimization_barrier((mine, other, values))
                self.trail.append((mine, other))
                return values

            def finish(self, spans):
                while len(self.trail) < fsdp:
                    self.turn()
                pieces = [piece for pair in self.trail for piece in pair]
                if all(size % 128 == 0 for size in spans):
                    return assemble(piece_places, pieces, spans)
                (full,) = assemble(piece_places, pieces, [sum(spans)])
                stops = [sum(spans[: i + 1]) for i in range(len(spans))]
                return [full[:, stop - size : stop] for size, stop in zip(spans, stops)]

        class ScatterRing:
            def __init__(self, blocks):
                self.blocks = blocks
                self.theirs, self.mine = blocks[fsdp - 1, 0], blocks[1 % fsdp, 1]
                self.step = 1

            def send(self):
                moved = [lax.ppermute(self.mine, "fsdp", backward_ring)]
                if self.step < fsdp - 1:
                    moved.append(lax.ppermute(self.theirs, "fsdp", onward))
                else:
                    moved.append(lax.ppermute(self.theirs, ("fsdp", "ctx"), on_across))
                if self.step == fsdp - 2:
                    moved.append(ctx_swap(self.blocks[0, 0]))
                return moved

            def add(self, moved):
                if self.step == fsdp - 2:
                    self.swapped = moved[2]
                more = self.blocks[(1 + self.step) % fsdp, 1]
                self.mine = (moved[0].astype(F32) + more.astype(F32)).astype(BF16)
                more = self.swapped if self.step == fsdp - 1 else self.blocks[fsdp - 1 - self.step, 0]
                self.theirs = (moved[1].astype(F32) + more.astype(F32)).astype(BF16)
                self.step += 1

        waiting = []

        def launch(rider):
            waiting.extend(advance(rider, None))

        def turn(rings, values=()):
            rings = [ring for ring in rings if ring.step < fsdp]
            due = [item for item in waiting if item[2] <= 1]
            waiting[:] = [(rider, v, left - 1) for rider, v, left in waiting if left > 1]
            moved, arrived, values = lax.optimization_barrier(
                ([ring.send() for ring in rings], [value for _, value, _ in due], values)
            )
            for ring, pair in zip(rings, moved):
                ring.add(pair)
            for item, value in zip(due, arrived):
                waiting.extend(advance(item[0], value))
            return values

        def finish(rings):
            while waiting or any(ring.step < fsdp for ring in rings):
                turn(rings)

        mine, other = pack(
            which,
            [
                jnp.transpose(self_weights, (1, 0, 2)),
                jnp.transpose(cross_memory, (1, 0, 2)),
                self_output.T[None],
                cross_query[None],
                cross_output.T[None],
            ],
        )
        ring = GatherRing(mine, other)
        trail = ring.trail
        w_qkv, w_memory, w_self_out, w_query, w_cross_out = ring.finish(
            [3 * q_self, 2 * q_self, q_self, q_self, q_self]
        )
        token_half = half_of(after(inputs[0], trail[1]))
        frames_here = after(encoder_states[0], trail[2])
        mine, other = pack(which, [hidden_in[None], hidden_out.T[None]])
        hidden_ring = GatherRing(*after((mine, other), trail[fsdp - 2]))
        cot_here = after(cotangent[0], trail[-2])
        def my_bias(bias):
            return lax.dynamic_index_in_dim(
                bias.reshape(bias.shape[:-1] + (ctx, -1)), c, bias.ndim - 1, keepdims=False
            )

        head_bias = my_bias(head_biases)
        hidden_own_bias = my_bias(hidden_bias)

        tokens = all_halves(token_half).astype(F32)
        frame_rows = frames_here.shape[0]
        frame_half = -(-frame_rows // 256) * 256
        piece = ctx_swap(
            lax.dynamic_slice_in_dim(frames_here, t * (width // tp), width // tp, axis=1)
        )
        if tp == 2:
            frames_there = ordered(piece, tp_swap(piece), t, 1)
        else:
            frames_there = lax.all_gather(piece, "tp", axis=1, tiled=True)
        blank = ((0, frame_half - frame_rows), (0, 0))
        frames = jnp.concatenate((jnp.pad(frames_here, blank), jnp.pad(frames_there, blank)), axis=0)
        cot_half = half_of(cot_here)
        cot_all = all_halves(cot_half)
        stream_half = own_half(tokens)

        normed_one, hat_one, inverse_one = layer_norm(tokens, norm_gains[0], norm_shifts[0])
        normed_one = normed_one.astype(BF16)
        projected = mm(normed_one, w_qkv, 1, 0)
        (projected,) = hidden_ring.turn((projected,))
        queries = (projected[:, :q_self] + head_bias[0]).astype(BF16)
        self_keys = projected[:, q_self : 2 * q_self].astype(BF16)
        self_values = (projected[:, 2 * q_self :] + head_bias[1]).astype(BF16)
        j = jnp.arange(ctx * rows, dtype=jnp.int32)
        jt, jc, i = j // half_rows, (j // part) % ctx, j % part
        if tp == 2:
            jt = jt ^ t
        position = jc * rows + jt * part + i
        places = (position[:, None], position[None, :])
        self_mixed, self_exact, self_totals = attend_forward(
            queries, self_keys, self_values, ctx * rows, ctx * rows, places
        )
        memory_bias = jnp.concatenate((jnp.zeros((q_self,), F32), head_bias[3]))
        frame_proj = (mm(frames, w_memory, 1, 0) + memory_bias).astype(BF16)
        (frame_proj,) = hidden_ring.turn((frame_proj,))
        after_self = stream_half + (
            group_sum(mm(self_mixed, w_self_out, 1, 1))
            + output_biases[0]
        )
        (after_self,) = hidden_ring.turn((after_self,))
        normed_two, hat_two, inverse_two = layer_norm(after_self, norm_gains[1], norm_shifts[1])
        normed_two = all_halves(normed_two.astype(BF16))
        cross_queries = (mm(normed_two, w_query, 1, 0) + head_bias[2]).astype(BF16)
        frame_keys, frame_values = frame_proj[:, :q_self], frame_proj[:, q_self:]
        cross_mixed, cross_exact, cross_totals = attend_forward(
            cross_queries, frame_keys, frame_values, frame_rows, frame_half
        )
        (cross_mixed,) = hidden_ring.turn((cross_mixed,))
        after_cross = after_self + (
            group_sum(mm(cross_mixed, w_cross_out, 1, 1)) + output_biases[1]
        )
        normed_three, hat_three, inverse_three = layer_norm(
            after_cross, norm_gains[2], norm_shifts[2]
        )
        normed_three = all_halves(normed_three.astype(BF16))
        w_in, w_out = hidden_ring.finish([q_hidden, q_hidden])
        pre_gelu = mm(normed_three, w_in, 1, 0) + hidden_own_bias
        cdf = 0.5 * (1.0 + lax.erf(pre_gelu * (0.5**0.5)))
        activated = (pre_gelu * cdf).astype(BF16)
        slope = cdf + pre_gelu * jnp.exp(-0.5 * pre_gelu * pre_gelu) * 0.3989422804014327

        grad_pre = (mm(cot_all, w_out, 1, 0) * slope).astype(BF16)
        grad_three = group_sum(mm(grad_pre, w_in, 1, 1))
        hidden_total = group_sum(mm(activated, w_out, 1, 1))
        output_half = (after_cross + (hidden_total + output_biases[2])).astype(BF16)
        layer_output = chip_rows(output_half)[None]
        done = {}
        grad_hidden = weight_grads(ring_order, which, [(normed_three, grad_pre), (cot_all, activated)])
        hidden_ring = ScatterRing(grad_hidden)
        grad_three = after(grad_three, grad_hidden)
        grad_after_cross = cot_half.astype(F32) + norm_back(
            hat_three, inverse_three, norm_gains[2], grad_three
        )
        grad_cross_half = grad_after_cross.astype(BF16)
        grad_cross = all_halves(grad_cross_half)

        grad_cross_mixed = mm(grad_cross, w_cross_out, 1, 0).astype(BF16)
        cross_grads = ()
        for only in range(max(1, q_self // 128)):
            cross_grads = attend_backward(
                cross_queries,
                frame_keys,
                frame_values,
                grad_cross_mixed,
                cross_exact,
                cross_totals,
                frame_rows,
                frame_half,
                only=only,
                into=tuple(cross_grads),
            )
            cross_grads = turn([hidden_ring], tuple(cross_grads))
        grad_cross_queries, grad_fkeys, grad_fvalues = cross_grads
        grad_two = group_sum(mm(grad_cross_queries, w_query, 1, 1))
        grad_frames = jnp.concatenate((grad_fkeys, grad_fvalues), axis=1)
        cross_blocks = weight_grads(
            ring_order,
            which,
            [(frames, grad_frames), (grad_cross, cross_mixed), (normed_two, grad_cross_queries)],
            columns=2,
        )
        (grad_two,) = turn([hidden_ring], (after(grad_two, cross_blocks),))
        grad_after_self = grad_after_cross + norm_back(
            hat_two, inverse_two, norm_gains[1], grad_two
        )
        grad_self_half = grad_after_self.astype(BF16)
        grad_self = all_halves(grad_self_half)

        grad_self_mixed = mm(grad_self, w_self_out, 1, 0).astype(BF16)
        grad_queries, grad_keys, grad_values = attend_backward(
            queries,
            self_keys,
            self_values,
            grad_self_mixed,
            self_exact,
            self_totals,
            ctx * rows,
            ctx * rows,
            places,
        )
        (grad_queries,) = turn([hidden_ring], (grad_queries,))
        grad_projected = jnp.concatenate((grad_queries, grad_keys, grad_values), axis=1)
        self_blocks = weight_grads(
            ring_order,
            which,
            [(normed_one, grad_projected), (grad_self, self_mixed)],
            columns=2,
            into=cross_blocks,
        )

        def column_sum(values):
            return jnp.sum(values.astype(F32), axis=0)

        def tokens_rider():
            partial = mm(grad_projected, w_qkv, 1, 1)
            if tp == 2:
                moved = yield tp_swap(partial[half_rows:].astype(BF16)), 1
                mine = (partial[:half_rows] + moved.astype(F32)).astype(BF16)
            else:
                mine = lax.psum_scatter(
                    partial.astype(BF16), "tp", scatter_dimension=0, tiled=True
                )
            moved = yield ctx_swap(mine), 2
            grad_one = mine.astype(F32) + moved.astype(F32)
            hat, inverse = own_half(hat_one), own_half(inverse_one)
            total = own_part(grad_after_self + norm_back(hat, inverse, norm_gains[0], grad_one))
            wide = jnp.stack(
                (
                    column_sum(grad_one * hat),
                    column_sum(hat_two * grad_two),
                    column_sum(hat_three * grad_three),
                    column_sum(grad_one),
                    column_sum(grad_two),
                    column_sum(grad_three),
                    column_sum(grad_self_half),
                    column_sum(grad_cross_half),
                    column_sum(cot_half),
                )
            )
            if tp == 2:
                moved, other_rows = yield (tp_swap(wide), tp_swap(total)), 1
                wide = wide + moved
                done["inputs"] = ordered(total, other_rows, t, 0)[None]
            else:
                wide = lax.psum(wide, "tp")
                done["inputs"] = lax.all_gather(total, "tp", axis=0, tiled=True)[None]
            narrow = jnp.concatenate(
                (
                    column_sum(grad_queries),
                    column_sum(grad_values),
                    column_sum(grad_cross_queries),
                    column_sum(grad_fvalues),
                    column_sum(grad_pre),
                )
            )
            small = jnp.concatenate((wide.reshape(-1), narrow))
            hop = 1
            while hop < fsdp:
                moved = yield lax.ppermute(small, "fsdp", [(i, i ^ hop) for i in range(fsdp)]), 1
                small = small + moved
                hop *= 2
            done["wide"] = small[: 9 * width].reshape(9, width)
            narrow = small[9 * width :]
            moved = yield ctx_swap(narrow), 1
            done["narrow"] = ordered(narrow[None], moved[None], c, 0)

        ring = ScatterRing(self_blocks)
        def frames_rider():
            encoder_part = mm(grad_frames, w_memory, 1, 1).astype(BF16)
            if tp == 2:
                half = width // 2
                keep = lax.dynamic_slice_in_dim(encoder_part, t * half, half, axis=1)
                give = lax.dynamic_slice_in_dim(encoder_part, (1 - t) * half, half, axis=1)
                moved = yield tp_swap(give), 1
                total = (keep.astype(F32) + moved.astype(F32)).astype(BF16)
            else:
                total = lax.psum_scatter(encoder_part, "tp", scatter_dimension=1, tiled=True)
            moved = yield ctx_swap(total[frame_half : frame_half + frame_rows]), 3
            done["frames"] = (total[:frame_rows].astype(F32) + moved.astype(F32))[None]

        launch(tokens_rider())
        launch(frames_rider())
        finish([hidden_ring, ring])
        grad_hidden_in, grad_hidden_out = unpack(
            which,
            hidden_ring.mine,
            hidden_ring.theirs,
            [(1, q_hidden), (1, q_hidden)],
        )
        (
            grad_self_weights,
            grad_self_output,
            grad_memory,
            grad_cross_output,
            grad_cross_query,
        ) = unpack(
            which,
            ring.mine,
            ring.theirs,
            [(3, q_self), (1, q_self), (2, q_self), (1, q_self), (1, q_self)],
        )
        grad_inputs, grad_encoder, wide = done["inputs"], done["frames"], done["wide"]
        both = done["narrow"]
        grad_head = both[:, : 4 * q_self].reshape(ctx, 4, q_self)
        grad_head = jnp.transpose(grad_head, (1, 0, 2)).reshape(4, -1)
        grad_hidden_bias = both[:, 4 * q_self :].reshape(-1)
        return (
            layer_output,
            grad_inputs,
            grad_encoder,
            jnp.transpose(grad_self_weights, (1, 0, 2)),
            grad_self_output[0].T,
            grad_cross_query[0],
            jnp.transpose(grad_memory, (1, 0, 2)),
            grad_cross_output[0].T,
            grad_hidden_in[0],
            grad_hidden_out[0].T,
            wide[0:3],
            wide[3:6],
            grad_head,
            wide[6:9],
            grad_hidden_bias,
        )

    return per_device


def solution(mesh):
    in_specs = (
        P("fsdp", "ctx", None),
        P("fsdp", "ctx", None),
        P(("fsdp", "ctx"), None, "tp"),
        P("tp", ("fsdp", "ctx")),
        P(("fsdp", "ctx"), "tp"),
        P(("fsdp", "ctx"), None, "tp"),
        P("tp", ("fsdp", "ctx")),
        P(("fsdp", "ctx"), "tp"),
        P("tp", ("fsdp", "ctx")),
        P(),
        P(),
        P(None, "tp"),
        P(),
        P("tp"),
        P("fsdp", "ctx", None),
    )
    out_specs = (
        P("fsdp", "ctx", None),
        P("fsdp", "ctx", None),
        P("fsdp", "ctx", "tp"),
        P(("fsdp", "ctx"), None, "tp"),
        P("tp", ("fsdp", "ctx")),
        P(("fsdp", "ctx"), "tp"),
        P(("fsdp", "ctx"), None, "tp"),
        P("tp", ("fsdp", "ctx")),
        P(("fsdp", "ctx"), "tp"),
        P("tp", ("fsdp", "ctx")),
        P(),
        P(),
        P(None, "tp"),
        P(),
        P("tp"),
    )
    per_device = build(mesh.shape["fsdp"], mesh.shape["ctx"], mesh.shape["tp"])
    return jax.shard_map(
        per_device, mesh=mesh, in_specs=in_specs, out_specs=out_specs, check_vma=False
    )
```

```python
import functools

import jax
import jax.numpy as jnp
from jax import lax
from jax.experimental import pallas as pl
from jax.experimental.pallas import tpu as pltpu
from jax.sharding import PartitionSpec as P

HEAD_DIM = 64
SCALING = HEAD_DIM ** (-0.5)
F32 = jnp.float32
BF16 = jnp.bfloat16


def key_tile(total):
    return 256 if total % 256 == 0 else total

def mm(left, right, left_dim, right_dim):
    return lax.dot_general(
        left, right, (((left_dim,), (right_dim,)), ((), ())), preferred_element_type=F32
    )

def only_head(values, head, group):
    if group == HEAD_DIM: return values
    lane = lax.broadcasted_iota(jnp.int32, values.shape, 1)
    return jnp.where(lane // HEAD_DIM == head, values, jnp.zeros_like(values))

def visible(tile, queries, start, used, half, key_place, query_place):
    if key_place is not None:
        return key_place[start:start+tile, :] <= query_place[...]
    row = start % half
    if row + tile > used:
        return row + lax.broadcasted_iota(jnp.int32, (tile, queries), 0) < used
    return None

def forward_kernel(used, half, causal, *refs):
    if causal:
        kp, qp, q_ref, k_ref, v_ref, mixed_ref, exact_ref, totals_ref = refs
    else:
        q_ref, k_ref, v_ref, mixed_ref, exact_ref, totals_ref = refs; kp = qp = None
    keys, group = k_ref.shape; queries = q_ref.shape[0]; tile = key_tile(keys)
    heads = group // HEAD_DIM
    q = (q_ref[...].astype(F32) * SCALING).astype(BF16)
    starts = range(0, keys, tile)
    qs = [only_head(q, h, group) for h in range(heads)]
    scores = [[None] * len(starts) for _ in range(heads)]
    tops = [None] * heads
    for i, start in enumerate(starts):
        ok = visible(tile, queries, start, used, half, kp, qp)
        for h in range(heads):
            s = mm(k_ref[start:start+tile, :], qs[h], 1, 1)
            if ok is not None: s = jnp.where(ok, s, -1e30)
            m = jnp.max(s, axis=0, keepdims=True)
            tops[h] = m if tops[h] is None else jnp.maximum(tops[h], m)
            scores[h][i] = s
    totals = [None] * heads; accs = [None] * heads
    for i, start in enumerate(starts):
        for h in range(heads):
            e = jnp.exp(scores[h][i] - tops[h])
            es = jnp.sum(e, axis=0, keepdims=True)
            o = mm(v_ref[start:start+tile, :], e.astype(BF16), 0, 0)
            totals[h] = es if totals[h] is None else totals[h] + es
            accs[h] = o if accs[h] is None else accs[h] + o
    for h in range(heads):
        rows = slice(h*HEAD_DIM, (h+1)*HEAD_DIM)
        exact_ref[rows, :] = accs[h][rows, :] * (1.0/totals[h])
        totals_ref[0, h:h+1, :] = tops[h] + jnp.log(totals[h])
    mixed_ref[...] = exact_ref[...].T.astype(BF16)

def backward_kernel(used, half, causal, kept, *refs):
    refs = refs[: len(refs) - 3 - kept] + refs[len(refs) - 3 :]
    if causal:
        kp, qp, q_ref, k_ref, v_ref, g_ref, exact_ref, totals_ref, dq_ref, dk_ref, dv_ref = refs
    else:
        q_ref, k_ref, v_ref, g_ref, exact_ref, totals_ref, dq_ref, dk_ref, dv_ref = refs; kp = qp = None
    keys, group = k_ref.shape; queries = q_ref.shape[0]; tile = key_tile(keys)
    heads = group // HEAD_DIM
    q = (q_ref[...].astype(F32) * SCALING).astype(BF16)
    g = g_ref[...]
    both = exact_ref[...] * g.astype(F32).T
    qs = [only_head(q, h, group) for h in range(heads)]
    gs = [only_head(g, h, group) for h in range(heads)]
    dots = [jnp.sum(both[h*HEAD_DIM:(h+1)*HEAD_DIM, :], axis=0, keepdims=True) for h in range(heads)]
    dqs = [None]*heads
    for start in range(0, keys, tile):
        k = k_ref[start:start+tile, :]; v = v_ref[start:start+tile, :]
        ok = visible(tile, queries, start, used, half, kp, qp)
        dk = dv = None
        for h in range(heads):
            s = mm(k, qs[h], 1, 1)
            if ok is not None: s = jnp.where(ok, s, -1e30)
            p = jnp.exp(s - totals_ref[0, h:h+1, :])
            dp = mm(v, gs[h], 1, 1)
            ds = (p * (dp - dots[h])).astype(BF16)
            a = mm(ds, qs[h], 1, 0); b = mm(p.astype(BF16), gs[h], 1, 0)
            dk = a if dk is None else dk + a
            dv = b if dv is None else dv + b
            c = mm(k, ds, 0, 0)
            dqs[h] = c if dqs[h] is None else dqs[h] + c
        dk_ref[start:start+tile, :] = dk.astype(BF16)
        dv_ref[start:start+tile, :] = dv.astype(BF16)
    full = jnp.concatenate([dqs[h][h*HEAD_DIM:(h+1)*HEAD_DIM, :] for h in range(heads)], axis=0)
    dq_ref[...] = (full.T * SCALING).astype(BF16)

def attend_forward(q, k, v, used, half, places=None):
    queries, width = q.shape; keys = k.shape[0]; group = min(128, width); n = width//group
    col = lambda rows: pl.BlockSpec((rows, group), lambda i: (0, i))
    fixed = lambda shape: pl.BlockSpec(shape, lambda i: (0, 0))
    extra = [] if places is None else list(places)
    return pl.pallas_call(
        functools.partial(forward_kernel, used, half, places is not None),
        grid=(n,),
        in_specs=[fixed(p.shape) for p in extra]+[col(queries), col(keys), col(keys)],
        out_specs=[col(queries), pl.BlockSpec((group, queries), lambda i: (i, 0)), pl.BlockSpec((1, group//HEAD_DIM, queries), lambda i: (i,0,0))],
        out_shape=[jax.ShapeDtypeStruct((queries,width),BF16), jax.ShapeDtypeStruct((width,queries),F32), jax.ShapeDtypeStruct((n,group//HEAD_DIM,queries),F32)],
        compiler_params=pltpu.CompilerParams(vmem_limit_bytes=20 * 2**20),
    )(*extra, q, k, v)

def attend_backward(q, k, v, g, exact, totals, used, half, places=None, only=None, into=()):
    queries, width = q.shape
    keys, group = k.shape[0], min(128, width)
    count = width // group
    first = 0 if only is None else only

    def columns(rows):
        return pl.BlockSpec((rows, group), lambda i: (0, first + i))

    def fixed(shape):
        return pl.BlockSpec(shape, lambda i: (0, 0))

    extra = [] if places is None else list(places)
    operands = [*extra, q, k, v, g, exact, totals]
    shapes = [(queries, width), (keys, width), (keys, width)]
    return pl.pallas_call(
        functools.partial(backward_kernel, used, half, places is not None, len(into)),
        grid=(count if only is None else 1,),
        in_specs=[fixed(place.shape) for place in extra]
        + [columns(queries), columns(keys), columns(keys), columns(queries)]
        + [pl.BlockSpec((group, queries), lambda i: (first + i, 0))]
        + [pl.BlockSpec((1, group // HEAD_DIM, queries), lambda i: (first + i, 0, 0))]
        + [pl.BlockSpec(memory_space=pl.ANY)] * len(into),
        out_specs=[columns(rows) for rows, _ in shapes],
        out_shape=[jax.ShapeDtypeStruct(shape, BF16) for shape in shapes],
        input_output_aliases={len(operands) + i: i for i in range(len(into))},
        compiler_params=pltpu.CompilerParams(vmem_limit_bytes=20 * 2**20),
    )(*operands, *into)


def weight_grads_kernel(count, order_ref, which_ref, *refs):
    out_ref, start = refs[-1], 0
    rows = out_ref.shape[2]
    step = pl.program_id(0)
    for i in range(count):
        left, right = refs[i], refs[count + i]
        stop = start + right.shape[1]
        total = mm(left[...], right[...], 0, 0).astype(BF16)
        devices = total.shape[0] // (2 * rows)
        for j in range(devices):
            place = order_ref[step * devices + j]
            for half in range(2):
                row = (2 * j + half) * rows
                out_ref[place, (which_ref[0] == half).astype(jnp.int32), :, start:stop] = total[
                    row : row + rows, :
                ]
        start = stop


def weight_grads(order, which, pairs, columns=1, into=None):
    steps, width = order.shape[0], pairs[0][0].shape[1]
    rows, total = width // steps, sum(right.shape[1] for _, right in pairs)
    count, tile = len(pairs), max(256, rows)
    out = (steps, 2, rows // 2, total * columns)
    column = columns - 1 if into is None else 0
    kept = () if into is None else (into,)
    return pl.pallas_call(
        functools.partial(weight_grads_kernel, count),
        grid_spec=pltpu.PrefetchScalarGridSpec(
            num_scalar_prefetch=2,
            grid=(width // tile,),
            in_specs=[
                pl.BlockSpec((left.shape[0], tile), lambda i, order, which: (0, i))
                for left, _ in pairs
            ]
            + [pl.BlockSpec(right.shape, lambda i, order, which: (0, 0)) for _, right in pairs]
            + [pl.BlockSpec(memory_space=pl.ANY)] * len(kept),
            out_specs=pl.BlockSpec(
                out[:3] + (total,), lambda i, order, which: (0, 0, 0, column)
            ),
        ),
        out_shape=jax.ShapeDtypeStruct(out, BF16),
        input_output_aliases={2 + 2 * count: 0} if kept else {},
        compiler_params=pltpu.CompilerParams(vmem_limit_bytes=20 * 2**20),
    )(order, which, *[left for left, _ in pairs], *[right for _, right in pairs], *kept)


def ring_add_kernel(counts, *refs):
    ins, outs = refs[: len(refs) - len(counts)], refs[len(refs) - len(counts) :]
    at = 0
    for count, out_ref in zip(counts, outs):
        moved, start = ins[at], 0
        for part in ins[at + 1 : at + 1 + count]:
            stop = start + part.shape[1]
            total = moved[:, start:stop].astype(F32) + part[...].astype(F32)
            out_ref[:, start:stop] = total.astype(BF16)
            start = stop
        at += 1 + count


def ring_add(items):
    specs, operands = [], []
    for moved, parts, distance, half in items:
        specs.append(pl.BlockSpec(memory_space=pltpu.VMEM))
        operands.append(moved)
        for part in parts:
            block = (None, None) + part.shape[2:]
            specs.append(pl.BlockSpec(block, lambda i, d=distance, h=half: (d, h, 0, 0)))
            operands.append(part)
    return pl.pallas_call(
        functools.partial(ring_add_kernel, [len(parts) for _, parts, _, _ in items]),
        grid=(1,),
        in_specs=specs,
        out_specs=[pl.BlockSpec(memory_space=pltpu.VMEM)] * len(items),
        out_shape=[jax.ShapeDtypeStruct(moved.shape, BF16) for moved, _, _, _ in items],
        compiler_params=pltpu.CompilerParams(vmem_limit_bytes=6 * 2**20),
    )(*operands)


def pack_kernel(count, which_ref, *refs):
    mine_ref, other_ref = refs[count:]
    for mine in range(2):

        @pl.when(which_ref[0] == mine)
        def _():
            start = 0
            for ref in refs[:count]:
                size = ref.shape[2] // 2
                for k in range(ref.shape[0]):
                    piece = ref[k]
                    for out_ref, index in ((mine_ref, mine), (other_ref, 1 - mine)):
                        out_ref[:, start : start + size] = piece[:, index * size : (index + 1) * size]
                    start += size


def pack(which, weights):
    rows = weights[0].shape[1]
    total = sum(weight.shape[0] * (weight.shape[2] // 2) for weight in weights)
    shape = jax.ShapeDtypeStruct((rows, total), BF16)
    return pl.pallas_call(
        functools.partial(pack_kernel, len(weights)),
        in_specs=[pl.BlockSpec(memory_space=pltpu.SMEM)]
        + [pl.BlockSpec(memory_space=pltpu.VMEM)] * len(weights),
        out_specs=[pl.BlockSpec(memory_space=pltpu.VMEM)] * 2,
        out_shape=[shape, shape],
        compiler_params=pltpu.CompilerParams(vmem_limit_bytes=6 * 2**20),
    )(which, *weights)


def unpack_kernel(counts, which_ref, mine_ref, theirs_ref, *out_refs):
    for mine in range(2):

        @pl.when(which_ref[0] == mine)
        def _():
            start = 0
            for ref, count in zip(out_refs, counts):
                size = ref.shape[2] // 2
                for k in range(count):
                    for in_ref, index in ((mine_ref, mine), (theirs_ref, 1 - mine)):
                        ref[k, :, index * size : (index + 1) * size] = in_ref[
                            :, start : start + size
                        ].astype(F32)
                    start += size


def unpack(which, mine, theirs, spans):
    rows = mine.shape[0]
    return pl.pallas_call(
        functools.partial(unpack_kernel, [count for count, _ in spans]),
        in_specs=[pl.BlockSpec(memory_space=pltpu.SMEM)]
        + [pl.BlockSpec(memory_space=pltpu.VMEM)] * 2,
        out_specs=[pl.BlockSpec(memory_space=pltpu.VMEM)] * len(spans),
        out_shape=[jax.ShapeDtypeStruct((count, rows, 2 * size), F32) for count, size in spans],
        compiler_params=pltpu.CompilerParams(vmem_limit_bytes=6 * 2**20),
    )(which, mine, theirs)


def assemble_kernel(count, spans, places_ref, *refs):
    pieces, outs, sems = refs[:count], refs[count:-1], refs[-1]
    rows = pieces[0].shape[0]

    def copies():
        for i in range(count):
            row = pl.multiple_of(places_ref[i] * rows, rows)
            start = 0
            for k, (size, out_ref) in enumerate(zip(spans, outs)):
                yield pltpu.make_async_copy(
                    pieces[i].at[:, start : start + size],
                    out_ref.at[pl.ds(row, rows), :],
                    sems.at[i * len(spans) + k],
                )
                start += size

    for copy in copies():
        copy.start()
    for copy in copies():
        copy.wait()


def assemble(places, pieces, spans):
    rows, count = pieces[0].shape[0], len(pieces)
    return pl.pallas_call(
        functools.partial(assemble_kernel, count, spans),
        in_specs=[pl.BlockSpec(memory_space=pltpu.SMEM)]
        + [pl.BlockSpec(memory_space=pl.ANY)] * count,
        out_specs=[pl.BlockSpec(memory_space=pltpu.VMEM)] * len(spans),
        out_shape=[jax.ShapeDtypeStruct((rows * count, size), BF16) for size in spans],
        scratch_shapes=[pltpu.SemaphoreType.DMA((count * len(spans),))],
        compiler_params=pltpu.CompilerParams(vmem_limit_bytes=16 * 2**20),
    )(places, *pieces)


def layer_norm(values, scales, shifts):
    row_mean = jnp.mean(values, axis=-1, keepdims=True)
    centred = values - row_mean
    variance = jnp.mean(centred * centred, axis=-1, keepdims=True)
    inverse = lax.rsqrt(variance + 1e-05)
    hat = centred * inverse
    return hat * scales + shifts, hat, inverse


def norm_back(hat, inverse, scales, incoming):
    scaled = incoming * scales
    return (
        scaled
        - jnp.mean(scaled, axis=-1, keepdims=True)
        - hat * jnp.mean(scaled * hat, axis=-1, keepdims=True)
    ) * inverse


def advance(rider, value):
    try:
        return [(rider,) + rider.send(value)]
    except StopIteration:
        return []


def build(fsdp, ctx, tp):
    assert ctx == 2
    ring = list(range(0, fsdp, 2)) + list(range(fsdp - 1, 0, -2)) if fsdp > 1 else [0]
    onward = [(ring[i], ring[(i + 1) % fsdp]) for i in range(fsdp)]
    backward_ring = [(b, a) for a, b in onward]
    swap = [(0, 1), (1, 0)]
    on_across = [(2 * a + c, 2 * b + 1 - c) for a, b in onward for c in range(2)]
    back_across = [(2 * a + c, 2 * b + 1 - c) for a, b in backward_ring for c in range(2)]

    def ring_place(index):
        return jnp.where(index % 2 == 0, index // 2, fsdp - 1 - index // 2)

    def ring_index(place):
        place = place % fsdp
        return jnp.where(2 * place < fsdp, 2 * place, 2 * fsdp - 1 - 2 * place)

    def ctx_swap(values):
        return lax.ppermute(values, "ctx", swap)

    def tp_swap(values):
        return lax.ppermute(values, "tp", swap)

    def ordered(first, second, index, axis):
        return jnp.where(
            index == 0,
            jnp.concatenate((first, second), axis=axis),
            jnp.concatenate((second, first), axis=axis),
        )

    def after(values, token):
        return lax.optimization_barrier((values, token))[0]

    def per_device(
        inputs,
        encoder_states,
        self_weights,
        self_output,
        cross_query,
        cross_memory,
        cross_output,
        hidden_in,
        hidden_out,
        norm_gains,
        norm_shifts,
        head_biases,
        output_biases,
        hidden_bias,
        cotangent,
    ):
        f, c, t = lax.axis_index("fsdp"), lax.axis_index("ctx"), lax.axis_index("tp")
        place = ring_place(f)
        rows, width = inputs.shape[1], inputs.shape[2]
        part = rows // tp
        half_rows = ctx * part
        shard = self_weights.shape[0]
        q_self = self_weights.shape[2] // ctx
        q_hidden = hidden_in.shape[1] // ctx

        def all_halves(half):
            if tp == 2:
                return jnp.concatenate((half, tp_swap(half)), axis=0)
            return lax.all_gather(half, "tp", axis=0, tiled=True)

        def own_half(values):
            if tp == 2:
                return values[:half_rows]
            return lax.dynamic_slice_in_dim(values, t * half_rows, half_rows, axis=0)

        def own_part(half):
            return lax.dynamic_slice_in_dim(half, c * part, part, axis=0)

        def group_sum(partial, hook=lambda mine: mine):
            if tp == 2:
                mine = partial[:half_rows] + tp_swap(partial[half_rows:].astype(BF16)).astype(F32)
            else:
                mine = lax.psum_scatter(
                    partial.astype(BF16), "tp", scatter_dimension=0, tiled=True
                )
            mine = hook(mine.astype(BF16))
            return mine.astype(F32) + ctx_swap(mine).astype(F32)

        def chip_rows(half):
            own = own_part(half)
            if tp == 2:
                return ordered(own, tp_swap(own), t, 0)
            return lax.all_gather(own, "tp", axis=0, tiled=True)

        def half_of(values):
            own = lax.dynamic_slice_in_dim(values, t * part, part, axis=0)
            return ordered(own, ctx_swap(own), c, 0)

        which = c.astype(jnp.int32).reshape(1)
        steps = jnp.arange(fsdp, dtype=jnp.int32)
        piece_places = jnp.stack(
            (
                ring_index(place + fsdp - steps) * ctx + c,
                ring_index(place + steps) * ctx + 1 - c,
            ),
            axis=1,
        ).reshape(-1)
        piece_places = piece_places.astype(jnp.int32)

        ring_order = ((ring_place(steps) - place) % fsdp).astype(jnp.int32)

        class GatherRing:
            def __init__(self, mine, other):
                self.first = (mine, other)
                self.trail = [(mine, ctx_swap(other))]

            def turn(self, values=()):
                if len(self.trail) == 1:
                    mine, other = self.first
                    other = lax.ppermute(other, ("fsdp", "ctx"), back_across)
                else:
                    mine, other = self.trail[-1]
                    other = lax.ppermute(other, "fsdp", backward_ring)
                mine = lax.ppermute(mine, "fsdp", onward)
                mine, other, values = lax.optimization_barrier((mine, other, values))
                self.trail.append((mine, other))
                return values

            def finish(self, spans):
                while len(self.trail) < fsdp:
                    self.turn()
                pieces = [piece for pair in self.trail for piece in pair]
                if all(size % 128 == 0 for size in spans):
                    return assemble(piece_places, pieces, spans)
                (full,) = assemble(piece_places, pieces, [sum(spans)])
                stops = [sum(spans[: i + 1]) for i in range(len(spans))]
                return [full[:, stop - size : stop] for size, stop in zip(spans, stops)]

        class ScatterRing:
            def __init__(self, blocks):
                self.blocks = blocks
                self.theirs, self.mine = blocks[fsdp - 1, 0], blocks[1 % fsdp, 1]
                self.step = 1

            def send(self):
                moved = [lax.ppermute(self.mine, "fsdp", backward_ring)]
                if self.step < fsdp - 1:
                    moved.append(lax.ppermute(self.theirs, "fsdp", onward))
                else:
                    moved.append(lax.ppermute(self.theirs, ("fsdp", "ctx"), on_across))
                if self.step == fsdp - 2:
                    moved.append(ctx_swap(self.blocks[0, 0]))
                return moved

            def add(self, moved):
                if self.step == fsdp - 2:
                    self.swapped = moved[2]
                more = self.blocks[(1 + self.step) % fsdp, 1]
                self.mine = (moved[0].astype(F32) + more.astype(F32)).astype(BF16)
                more = self.swapped if self.step == fsdp - 1 else self.blocks[fsdp - 1 - self.step, 0]
                self.theirs = (moved[1].astype(F32) + more.astype(F32)).astype(BF16)
                self.step += 1

        waiting = []

        def launch(rider):
            waiting.extend(advance(rider, None))

        def turn(rings, values=()):
            rings = [ring for ring in rings if ring.step < fsdp]
            due = [item for item in waiting if item[2] <= 1]
            waiting[:] = [(rider, v, left - 1) for rider, v, left in waiting if left > 1]
            moved, arrived, values = lax.optimization_barrier(
                ([ring.send() for ring in rings], [value for _, value, _ in due], values)
            )
            for ring, pair in zip(rings, moved):
                ring.add(pair)
            for item, value in zip(due, arrived):
                waiting.extend(advance(item[0], value))
            return values

        def finish(rings):
            while waiting or any(ring.step < fsdp for ring in rings):
                turn(rings)

        mine, other = pack(
            which,
            [
                jnp.transpose(self_weights, (1, 0, 2)),
                jnp.transpose(cross_memory, (1, 0, 2)),
                self_output.T[None],
                cross_query[None],
                cross_output.T[None],
            ],
        )
        ring = GatherRing(mine, other)
        trail = ring.trail
        w_qkv, w_memory, w_self_out, w_query, w_cross_out = ring.finish(
            [3 * q_self, 2 * q_self, q_self, q_self, q_self]
        )
        token_half = half_of(after(inputs[0], trail[1]))
        frames_here = after(encoder_states[0], trail[2])
        mine, other = pack(which, [hidden_in[None], hidden_out.T[None]])
        hidden_ring = GatherRing(*after((mine, other), trail[fsdp - 2]))
        cot_here = after(cotangent[0], trail[-2])
        def my_bias(bias):
            return lax.dynamic_index_in_dim(
                bias.reshape(bias.shape[:-1] + (ctx, -1)), c, bias.ndim - 1, keepdims=False
            )

        head_bias = my_bias(head_biases)
        hidden_own_bias = my_bias(hidden_bias)

        tokens = all_halves(token_half).astype(F32)
        frame_rows = frames_here.shape[0]
        frame_half = -(-frame_rows // 256) * 256
        piece = ctx_swap(
            lax.dynamic_slice_in_dim(frames_here, t * (width // tp), width // tp, axis=1)
        )
        if tp == 2:
            frames_there = ordered(piece, tp_swap(piece), t, 1)
        else:
            frames_there = lax.all_gather(piece, "tp", axis=1, tiled=True)
        blank = ((0, frame_half - frame_rows), (0, 0))
        frames = jnp.concatenate((jnp.pad(frames_here, blank), jnp.pad(frames_there, blank)), axis=0)
        cot_half = half_of(cot_here)
        cot_all = all_halves(cot_half)
        stream_half = own_half(tokens)

        normed_one, hat_one, inverse_one = layer_norm(tokens, norm_gains[0], norm_shifts[0])
        normed_one = normed_one.astype(BF16)
        projected = mm(normed_one, w_qkv, 1, 0)
        (projected,) = hidden_ring.turn((projected,))
        queries = (projected[:, :q_self] + head_bias[0]).astype(BF16)
        self_keys = projected[:, q_self : 2 * q_self].astype(BF16)
        self_values = (projected[:, 2 * q_self :] + head_bias[1]).astype(BF16)
        j = jnp.arange(ctx * rows, dtype=jnp.int32)
        jt, jc, i = j // half_rows, (j // part) % ctx, j % part
        if tp == 2:
            jt = jt ^ t
        position = jc * rows + jt * part + i
        places = (position[:, None], position[None, :])
        self_mixed, self_exact, self_totals = attend_forward(
            queries, self_keys, self_values, ctx * rows, ctx * rows, places
        )
        memory_bias = jnp.concatenate((jnp.zeros((q_self,), F32), head_bias[3]))
        frame_proj = (mm(frames, w_memory, 1, 0) + memory_bias).astype(BF16)
        (frame_proj,) = hidden_ring.turn((frame_proj,))
        after_self = stream_half + (
            group_sum(mm(self_mixed, w_self_out, 1, 1))
            + output_biases[0]
        )
        (after_self,) = hidden_ring.turn((after_self,))
        normed_two, hat_two, inverse_two = layer_norm(after_self, norm_gains[1], norm_shifts[1])
        normed_two = all_halves(normed_two.astype(BF16))
        cross_queries = (mm(normed_two, w_query, 1, 0) + head_bias[2]).astype(BF16)
        frame_keys, frame_values = frame_proj[:, :q_self], frame_proj[:, q_self:]
        cross_mixed, cross_exact, cross_totals = attend_forward(
            cross_queries, frame_keys, frame_values, frame_rows, frame_half
        )
        (cross_mixed,) = hidden_ring.turn((cross_mixed,))
        after_cross = after_self + (
            group_sum(mm(cross_mixed, w_cross_out, 1, 1)) + output_biases[1]
        )
        normed_three, hat_three, inverse_three = layer_norm(
            after_cross, norm_gains[2], norm_shifts[2]
        )
        normed_three = all_halves(normed_three.astype(BF16))
        w_in, w_out = hidden_ring.finish([q_hidden, q_hidden])
        pre_gelu = mm(normed_three, w_in, 1, 0) + hidden_own_bias
        cdf = 0.5 * (1.0 + lax.erf(pre_gelu * (0.5**0.5)))
        activated = (pre_gelu * cdf).astype(BF16)
        slope = cdf + pre_gelu * jnp.exp(-0.5 * pre_gelu * pre_gelu) * 0.3989422804014327

        grad_pre = (mm(cot_all, w_out, 1, 0) * slope).astype(BF16)
        grad_three = group_sum(mm(grad_pre, w_in, 1, 1))
        hidden_total = group_sum(mm(activated, w_out, 1, 1))
        output_half = (after_cross + (hidden_total + output_biases[2])).astype(BF16)
        layer_output = chip_rows(output_half)[None]
        done = {}
        grad_hidden = weight_grads(ring_order, which, [(normed_three, grad_pre), (cot_all, activated)])
        hidden_ring = ScatterRing(grad_hidden)
        grad_three = after(grad_three, grad_hidden)
        grad_after_cross = cot_half.astype(F32) + norm_back(
            hat_three, inverse_three, norm_gains[2], grad_three
        )
        grad_cross_half = grad_after_cross.astype(BF16)
        grad_cross = all_halves(grad_cross_half)

        grad_cross_mixed = mm(grad_cross, w_cross_out, 1, 0).astype(BF16)
        cross_grads = ()
        for only in range(max(1, q_self // 128)):
            cross_grads = attend_backward(
                cross_queries,
                frame_keys,
                frame_values,
                grad_cross_mixed,
                cross_exact,
                cross_totals,
                frame_rows,
                frame_half,
                only=only,
                into=tuple(cross_grads),
            )
            queries_part, *frame_parts = cross_grads
            frame_parts = turn([hidden_ring], tuple(frame_parts))
            cross_grads = (queries_part, *frame_parts)
        grad_cross_queries, grad_fkeys, grad_fvalues = cross_grads
        grad_two = group_sum(mm(grad_cross_queries, w_query, 1, 1))
        grad_frames = jnp.concatenate((grad_fkeys, grad_fvalues), axis=1)
        cross_blocks = weight_grads(
            ring_order,
            which,
            [(frames, grad_frames), (grad_cross, cross_mixed), (normed_two, grad_cross_queries)],
            columns=2,
        )
        (grad_two,) = turn([hidden_ring], (after(grad_two, cross_blocks),))
        grad_after_self = grad_after_cross + norm_back(
            hat_two, inverse_two, norm_gains[1], grad_two
        )
        grad_self_half = grad_after_self.astype(BF16)
        grad_self = all_halves(grad_self_half)

        grad_self_mixed = mm(grad_self, w_self_out, 1, 0).astype(BF16)
        grad_queries, grad_keys, grad_values = attend_backward(
            queries,
            self_keys,
            self_values,
            grad_self_mixed,
            self_exact,
            self_totals,
            ctx * rows,
            ctx * rows,
            places,
        )
        (grad_queries,) = turn([hidden_ring], (grad_queries,))
        grad_projected = jnp.concatenate((grad_queries, grad_keys, grad_values), axis=1)
        self_blocks = weight_grads(
            ring_order,
            which,
            [(normed_one, grad_projected), (grad_self, self_mixed)],
            columns=2,
            into=cross_blocks,
        )

        def column_sum(values):
            return jnp.sum(values.astype(F32), axis=0)

        def tokens_rider():
            partial = mm(grad_projected, w_qkv, 1, 1)
            if tp == 2:
                moved = yield tp_swap(partial[half_rows:].astype(BF16)), 1
                mine = (partial[:half_rows] + moved.astype(F32)).astype(BF16)
            else:
                mine = lax.psum_scatter(
                    partial.astype(BF16), "tp", scatter_dimension=0, tiled=True
                )
            moved = yield ctx_swap(mine), 2
            grad_one = mine.astype(F32) + moved.astype(F32)
            hat, inverse = own_half(hat_one), own_half(inverse_one)
            total = own_part(grad_after_self + norm_back(hat, inverse, norm_gains[0], grad_one))
            wide = jnp.stack(
                (
                    column_sum(grad_one * hat),
                    column_sum(hat_two * grad_two),
                    column_sum(hat_three * grad_three),
                    column_sum(grad_one),
                    column_sum(grad_two),
                    column_sum(grad_three),
                    column_sum(grad_self_half),
                    column_sum(grad_cross_half),
                    column_sum(cot_half),
                )
            )
            if tp == 2:
                moved, other_rows = yield (tp_swap(wide), tp_swap(total)), 1
                wide = wide + moved
                done["inputs"] = ordered(total, other_rows, t, 0)[None]
            else:
                wide = lax.psum(wide, "tp")
                done["inputs"] = lax.all_gather(total, "tp", axis=0, tiled=True)[None]
            narrow = jnp.concatenate(
                (
                    column_sum(grad_queries),
                    column_sum(grad_values),
                    column_sum(grad_cross_queries),
                    column_sum(grad_fvalues),
                    column_sum(grad_pre),
                )
            )
            small = jnp.concatenate((wide.reshape(-1), narrow))
            hop = 1
            while hop < fsdp:
                moved = yield lax.ppermute(small, "fsdp", [(i, i ^ hop) for i in range(fsdp)]), 1
                small = small + moved
                hop *= 2
            done["wide"] = small[: 9 * width].reshape(9, width)
            narrow = small[9 * width :]
            moved = yield ctx_swap(narrow), 1
            done["narrow"] = ordered(narrow[None], moved[None], c, 0)

        ring = ScatterRing(self_blocks)
        def frames_rider():
            encoder_part = mm(grad_frames, w_memory, 1, 1).astype(BF16)
            if tp == 2:
                half = width // 2
                keep = lax.dynamic_slice_in_dim(encoder_part, t * half, half, axis=1)
                give = lax.dynamic_slice_in_dim(encoder_part, (1 - t) * half, half, axis=1)
                moved = yield tp_swap(give), 1
                total = (keep.astype(F32) + moved.astype(F32)).astype(BF16)
            else:
                total = lax.psum_scatter(encoder_part, "tp", scatter_dimension=1, tiled=True)
            moved = yield ctx_swap(total[frame_half : frame_half + frame_rows]), 3
            done["frames"] = (total[:frame_rows].astype(F32) + moved.astype(F32))[None]

        launch(tokens_rider())
        launch(frames_rider())
        finish([hidden_ring, ring])
        grad_hidden_in, grad_hidden_out = unpack(
            which,
            hidden_ring.mine,
            hidden_ring.theirs,
            [(1, q_hidden), (1, q_hidden)],
        )
        (
            grad_self_weights,
            grad_self_output,
            grad_memory,
            grad_cross_output,
            grad_cross_query,
        ) = unpack(
            which,
            ring.mine,
            ring.theirs,
            [(3, q_self), (1, q_self), (2, q_self), (1, q_self), (1, q_self)],
        )
        grad_inputs, grad_encoder, wide = done["inputs"], done["frames"], done["wide"]
        both = done["narrow"]
        grad_head = both[:, : 4 * q_self].reshape(ctx, 4, q_self)
        grad_head = jnp.transpose(grad_head, (1, 0, 2)).reshape(4, -1)
        grad_hidden_bias = both[:, 4 * q_self :].reshape(-1)
        return (
            layer_output,
            grad_inputs,
            grad_encoder,
            jnp.transpose(grad_self_weights, (1, 0, 2)),
            grad_self_output[0].T,
            grad_cross_query[0],
            jnp.transpose(grad_memory, (1, 0, 2)),
            grad_cross_output[0].T,
            grad_hidden_in[0],
            grad_hidden_out[0].T,
            wide[0:3],
            wide[3:6],
            grad_head,
            wide[6:9],
            grad_hidden_bias,
        )

    return per_device


def solution(mesh):
    in_specs = (
        P("fsdp", "ctx", None),
        P("fsdp", "ctx", None),
        P(("fsdp", "ctx"), None, "tp"),
        P("tp", ("fsdp", "ctx")),
        P(("fsdp", "ctx"), "tp"),
        P(("fsdp", "ctx"), None, "tp"),
        P("tp", ("fsdp", "ctx")),
        P(("fsdp", "ctx"), "tp"),
        P("tp", ("fsdp", "ctx")),
        P(),
        P(),
        P(None, "tp"),
        P(),
        P("tp"),
        P("fsdp", "ctx", None),
    )
    out_specs = (
        P("fsdp", "ctx", None),
        P("fsdp", "ctx", None),
        P("fsdp", "ctx", "tp"),
        P(("fsdp", "ctx"), None, "tp"),
        P("tp", ("fsdp", "ctx")),
        P(("fsdp", "ctx"), "tp"),
        P(("fsdp", "ctx"), None, "tp"),
        P("tp", ("fsdp", "ctx")),
        P(("fsdp", "ctx"), "tp"),
        P("tp", ("fsdp", "ctx")),
        P(),
        P(),
        P(None, "tp"),
        P(),
        P("tp"),
    )
    per_device = build(mesh.shape["fsdp"], mesh.shape["ctx"], mesh.shape["tp"])
    return jax.shard_map(
        per_device, mesh=mesh, in_specs=in_specs, out_specs=out_specs, check_vma=False
    )
```
